32 devices in a mesh: grp: 2 (over y), seq: 16 (over z, x, core).
Axes of the slice: x: 2, y: 2, z: 4, core: 2. Of those that a mesh axis runs over, the one named last changes fastest.
Arguments:
- queries: bfloat16 [8192, 2048], P(('grp', 'seq')), parts along dimension 0, may hold values from -6 to 6
- keys: bfloat16 [8192, 2048], P(('grp', 'seq')), parts along dimension 0, may hold values from -6 to 6
- values: bfloat16 [8192, 2048], P(('grp', 'seq')), parts along dimension 0, may hold values from -6 to 6
- level_index: int32 [8192], P(('grp', 'seq')), parts along dimension 0, may hold values from 0 to 63
- level_table: float32 [64, 18, 16], replicated, may hold values from 0 to 10
- norm_gain: float32 [2048], replicated, may hold values from 0.1 to 1.9
- out_weight: bfloat16 [2048, 2048], P(None, 'seq'), may hold values from -0.125 to 0.125
Outputs:
- block_out: bfloat16 [8192, 2048], P(('grp', 'seq')), parts along dimension 0
The draws below stay inside these ranges and needn't reach their ends.
There are 2 independent parts, one for each index of `grp`. The reference program is written for one: setup_inputs(seed, part) draws one part's arguments, and reference() takes and returns one part's arrays. A program takes and returns all parts, laid end to end along the dimension named above; an argument that names none is the same for every part. Nothing has to cross between parts.
All inputs are finite; a program needn't handle non-finite values.
Results may differ from the reference program's by a relative error of at most 0.0057.
Values may be sent and summed in bfloat16 or wider, within the bound.
No kernel may reach another device: no remote copies, remote signals or barrier semaphores. Data moves between devices by JAX's collectives and lax.ppermute only.
A program may use at most 128 MiB of HBM per device.

```python
import math
import jax
import jax.numpy as jnp
from jax import lax

H = 16
NTAB = 64
LEVELS = 18
C = 256
D = 2048
LENGTH = 4096
N_SEQ = 16


def draw_level_table(key, part):
    lowest, highest = (math.log(0.2), math.log(5.0))
    base = jax.random.uniform(key, (NTAB, LEVELS, H), jnp.float32, lowest, highest)
    level = jnp.arange(LEVELS).astype(jnp.float32)
    shrink = jnp.exp2(-0.5 * jnp.maximum(level - 1.0, 0.0))
    return jnp.exp(base) * shrink[None, :, None]


def set_ends(values, own_key, smallest, high):
    index_at = [jax.random.randint(jax.random.fold_in(own_key, axis), (), 0, length) for axis, length in enumerate(values.shape)]
    widest = values.shape.index(max(values.shape))
    neighbour = index_at[:widest] + [(index_at[widest] + 1) % values.shape[widest]] + index_at[widest + 1:]
    return values.at[tuple(index_at)].set(smallest).at[tuple(neighbour)].set(high)


def shard_levels(stream_key, dims, cuts, least, largest):
    def one(position, shards_of):
        steps = jax.random.uniform(jax.random.fold_in(jax.random.fold_in(stream_key, 6), position), (shards_of,), jnp.float32, least / len(cuts), largest / len(cuts))
        return jnp.repeat(jnp.exp(steps), dims[position] // shards_of).reshape((-1,) + (1,) * (len(dims) - position - 1))

    level = one(*cuts[0])
    for cut in cuts[1:]:
        level = level * one(*cut)
    return level


def scatter_about(stream_key, shape, scale, limit, shards=(), held_as=jnp.bfloat16):
    drawn = scale * jax.random.normal(stream_key, shape, jnp.float32)
    if shards:
        drawn = drawn * shard_levels(stream_key, shape, shards, -0.22, 0.18)
    return jnp.clip(drawn, -limit, limit).astype(held_as)


def setup_inputs(seed: int = 0, part: int = 0) -> dict:
    key_list = jax.random.split(jax.random.key(seed), 8)
    part_keys = jax.random.split(jax.random.fold_in(key_list[7], part), 8)
    return {
        "queries": scatter_about(part_keys[0], (LENGTH, D), 1.0, 6.0, ((0, 16),)),
        "keys": scatter_about(part_keys[1], (LENGTH, D), 1.0, 6.0, ((0, 16),)),
        "values": scatter_about(part_keys[2], (LENGTH, D), 1.0, 6.0, ((0, 16),)),
        "level_index": set_ends(jax.random.randint(part_keys[3], (LENGTH,), 0, NTAB), jax.random.fold_in(part_keys[3], 1), 0, NTAB - 1).astype(jnp.int32),
        "level_table": draw_level_table(jax.random.fold_in(key_list[7], 71), part),
        "norm_gain": jnp.clip(1.0 + 0.18 * jax.random.normal(key_list[5], (D,), jnp.float32), 0.1, 1.9),
        "out_weight": scatter_about(key_list[6], (D, D), D ** -0.5, 0.125, ((1, 16),)),
    }


def reference(queries, keys, values, level_index, level_table, norm_gain, out_weight):
    heads = level_table.shape[2]
    width = queries.shape[1]
    head_dim = width // heads
    blocks = N_SEQ
    stretch = C
    log_stretch = stretch.bit_length() - 1
    log_blocks = blocks.bit_length() - 1
    scale = 1.0 / math.sqrt(head_dim)
    q_all = queries.reshape(blocks, stretch, heads, head_dim)
    k_all = keys.reshape(blocks, stretch, heads, head_dim)
    v_all = values.reshape(blocks, stretch, heads, head_dim)
    states = jnp.einsum('bshe,bshf->bhef', k_all.astype(jnp.float32), v_all.astype(jnp.float32))
    group_sums = []
    for level in range(log_blocks):
        group_sums.append(states.reshape(blocks >> level, 1 << level, heads, head_dim, head_dim).sum(axis=1))
    lam_all = level_table[level_index].reshape(blocks, stretch, level_table.shape[1], heads)
    positions = jnp.arange(stretch, dtype=jnp.int32)
    level_grid = jnp.zeros((stretch, stretch), jnp.int32)
    for bit in range(log_stretch):
        level_grid = level_grid + (jnp.right_shift(positions[:, None], bit) != jnp.right_shift(positions[None, :], bit)).astype(jnp.int32)
    causal = positions[None, :] <= positions[:, None]
    gain = norm_gain.reshape(heads, 1, head_dim)

    def one_block(block):
        q_blk = jnp.transpose(lax.dynamic_index_in_dim(q_all, block, 0, keepdims=False), (1, 0, 2)).astype(jnp.float32)
        k_blk = jnp.transpose(lax.dynamic_index_in_dim(k_all, block, 0, keepdims=False), (1, 0, 2)).astype(jnp.float32)
        v_blk = jnp.transpose(lax.dynamic_index_in_dim(v_all, block, 0, keepdims=False), (1, 0, 2)).astype(jnp.float32)
        lam_heads = jnp.transpose(lax.dynamic_index_in_dim(lam_all, block, 0, keepdims=False), (2, 0, 1))
        scores = jnp.einsum('hte,hse->hts', q_blk, k_blk) * scale
        picked = jnp.take_along_axis(lam_heads, jnp.broadcast_to(level_grid[None], (heads, stretch, stretch)), axis=2)
        weighted = jnp.where(causal[None], picked * scores, 0.0).astype(jnp.bfloat16)
        local = jnp.einsum('hts,hsf->htf', weighted.astype(jnp.float32), v_blk)
        far = jnp.zeros((heads, stretch, head_dim), jnp.float32)
        for level in range(log_blocks):
            owned = jnp.right_shift(block, level) % 2 == 1
            slot = jnp.maximum(jnp.right_shift(block, level) - 1, 0).astype(jnp.int32)
            bucket = lax.dynamic_index_in_dim(group_sums[level], slot, 0, keepdims=False).astype(jnp.bfloat16)
            term = jnp.einsum('hte,hef->htf', q_blk, bucket.astype(jnp.float32))
            weight = lam_heads[:, :, log_stretch + 1 + level:log_stretch + 2 + level]
            far = far + jnp.where(owned, weight * term * scale, 0.0)
        mixed = local + far
        normed = mixed * lax.rsqrt(lax.optimization_barrier(jnp.mean(mixed * mixed, axis=2, keepdims=True)) + 1e-06) * gain
        return jnp.transpose(normed, (1, 0, 2)).reshape(stretch, width).astype(jnp.bfloat16)
    normed_all = lax.map(one_block, jnp.arange(blocks, dtype=jnp.int32)).reshape(blocks * stretch, width)
    return jnp.dot(normed_all, out_weight, preferred_element_type=jnp.float32).astype(jnp.bfloat16)
```

```python
import functools
import math

import numpy as np

import jax
import jax.numpy as jnp
from jax import lax
from jax.experimental import pallas as pl
from jax.experimental.pallas import tpu as pltpu
from jax.sharding import PartitionSpec as P

TILE = 128
VM = pl.BlockSpec(memory_space=pltpu.VMEM)
SM = pl.BlockSpec(memory_space=pltpu.SMEM)
PARAMS = pltpu.CompilerParams(vmem_limit_bytes=8 * 1024 * 1024)


def call(kernel, out_shape, in_specs, flops, moved, *operands):
    outs = jax.tree.map(lambda _: VM, out_shape)
    return pl.pallas_call(
        kernel,
        out_shape=out_shape,
        in_specs=in_specs,
        out_specs=outs,
        compiler_params=PARAMS,
        cost_estimate=pl.CostEstimate(flops=flops, bytes_accessed=moved, transcendentals=0),
    )(*operands)


def lanes(start, size):
    return pl.ds(pl.multiple_of(start, TILE), size)


def dot(a, b, ca=1, cb=0):
    return lax.dot_general(a, b, (((ca,), (cb,)), ((), ())), preferred_element_type=jnp.float32)


def state_kernel(info, k_ref, v_ref, got_ref, sum_ref, send_ref, even_ref):
    heads, dim, _ = sum_ref.shape
    rows = k_ref.shape[0]
    core = info[0]
    for h in range(heads):
        own = lanes(core * heads * dim + h * dim, dim)
        far = pl.ds(h * dim, dim)
        mine = dot(k_ref[:, own], v_ref[:, own], 0, 0)
        theirs = dot(got_ref[pl.ds(0, rows), far], got_ref[pl.ds(rows, rows), far], 0, 0)
        both = mine + theirs
        sum_ref[h] = both
        send_ref[h] = both.astype(jnp.bfloat16)
        even_ref[h] = jnp.where(core == 0, mine, theirs).astype(jnp.bfloat16)


def pick_rows(index_ref, table, rows, start):
    found = index_ref[pl.ds(start, rows), :] == lax.broadcasted_iota(jnp.int32, (rows, table.shape[0]), 1)
    return lax.dot_general(
        found.astype(jnp.float32),
        table,
        (((1,), (0,)), ((), ())),
        precision=lax.Precision.HIGHEST,
        preferred_element_type=jnp.float32,
    )


def local_kernel(log_stretch, info, q_ref, k_ref, v_ref, got_ref, index_ref, table_ref, even_ref, out_ref):
    heads, dim = even_ref.shape[0], even_ref.shape[1]
    rows = q_ref.shape[0]
    core = info[0]
    scale = 1.0 / math.sqrt(dim)
    step = min(TILE, rows)
    t_at = lax.broadcasted_iota(jnp.int32, (step, step), 0)
    s_at = lax.broadcasted_iota(jnp.int32, (step, step), 1)
    grid = jnp.zeros((step, step), jnp.int32)
    log_step = step.bit_length() - 1
    for bit in range(log_step):
        grid = grid + (jnp.right_shift(t_at, bit) != jnp.right_shift(s_at, bit)).astype(jnp.int32)
    grid = jnp.where(s_at <= t_at, grid, -1)

    def one(h, _):
        own = lanes(core * heads * dim + h * dim, dim)
        far = lanes(h * dim, dim)
        table = table_ref[core * heads + h]
        for side in range(2):
            if side == 0:
                odd = core

                def part(which, block):
                    ref = (k_ref, v_ref, q_ref)[which]
                    return ref[pl.ds(block * step, step), own]
            else:
                odd = 1 - core

                def part(which, block):
                    return got_ref[pl.ds(which * rows + block * step, step), far]

            lam = pick_rows(index_ref, table, rows, side * rows) * scale
            for block in range(rows // step):
                lam_b = lam[block * step : (block + 1) * step]
                q = part(2, block)
                weight = jnp.where(odd == 1, lam_b[:, log_stretch + 1 : log_stretch + 2], 0.0)
                total = weight * dot(q, even_ref[h])
                for other in range(block + 1):
                    scores = dot(q, part(0, other), 1, 1)
                    if other == block:
                        picked = jnp.zeros((step, step), jnp.float32)
                        for level in range(log_step + 1):
                            picked = jnp.where(grid == level, lam_b[:, level : level + 1], picked)
                    else:
                        level = log_step + (block ^ other).bit_length()
                        picked = lam_b[:, level : level + 1]
                    total = total + dot((picked * scores).astype(jnp.bfloat16), part(1, other))
                out_ref[pl.ds(side * rows + block * step, step), far] = total
        return 0

    lax.fori_loop(0, heads, one, 0)


def far_kernel(levels, final, log_stretch, *refs):
    count = len(levels)
    info, q_ref, got_ref, index_ref, table_ref, base_ref = refs[:6]
    buckets = refs[6 : 6 + count]
    rows = q_ref.shape[0]
    heads = table_ref.shape[0] // 2
    dim = base_ref.shape[1] // heads
    core = info[0]
    scale = 1.0 / math.sqrt(dim)
    if final:
        gain_ref, out_ref = refs[6 + count :]
    else:
        (out_ref,) = refs[6 + count :]

    def one(h, _):
        own = lanes(core * heads * dim + h * dim, dim)
        far = lanes(h * dim, dim)
        table = table_ref[core * heads + h]
        for side in range(2):
            lam = pick_rows(index_ref, table, rows, side * rows)
            q = q_ref[:, own] if side == 0 else got_ref[pl.ds(2 * rows, rows), far]
            total = base_ref[pl.ds(side * rows, rows), far]
            for at, level in enumerate(levels):
                column = log_stretch + 1 + level
                weight = jnp.where(info[1 + level] == 1, lam[:, column : column + 1] * scale, 0.0)
                total = total + weight * dot(q, buckets[at][h])
            if final:
                mean = jnp.mean(total * total, axis=1, keepdims=True)
                total = total * lax.rsqrt(mean + 1e-06) * gain_ref[:, own]
            out_ref[pl.ds(side * rows, rows), far] = total.astype(out_ref.dtype)
        return 0

    lax.fori_loop(0, heads, one, 0)


def project_kernel(side, plan, info, normed_ref, *refs):
    out_ref = refs[-1]
    rows = out_ref.shape[0]
    for chip_slot, parts in plan:
        total = None
        for at, row0, k_slot, k_add, size in parts:
            piece = refs[at]
            start = k_add if k_slot is None else info[k_slot] + k_add
            a = normed_ref[pl.ds(side * rows, rows), lanes(start, size)]
            term = dot(a, piece[pl.ds(row0, size), :])
            total = term if total is None else total + term
        width = refs[parts[0][0]].shape[1]
        column = 0 if chip_slot is None else info[chip_slot] * width
        out_ref[:, lanes(column, width)] = total.astype(out_ref.dtype)


def ring_order(chips):
    return list(range(0, chips, 2)) + list(range(chips - 1, 0, -2))


def body(groups, queries, keys, values, level_index, level_table, norm_gain, out_weight):
    stretch, width = queries.shape
    table_rows, level_count, heads = level_table.shape
    head_dim = width // heads
    columns = out_weight.shape[1]
    log_stretch = stretch.bit_length() - 1
    devices = lax.axis_size("seq")
    log_blocks = devices.bit_length() - 1
    rank = lax.axis_index("seq")
    group = lax.axis_index("grp")
    core = rank % 2
    half = width // 2
    pair_heads = heads // 2
    chips = devices // 2
    ringed = (2 * columns) % TILE == 0 and chips >= 4
    shared = (3 * half // 8) // TILE * TILE if ringed and groups == 2 else 0
    kept = half - shared
    cut = kept // TILE // 2 * TILE

    order = ring_order(chips)
    facts = np.zeros((groups, devices, 1 + log_blocks + 2 + chips), np.int32)
    for g in range(groups):
        for r in range(devices):
            place = order.index(r // 2) if ringed else 0
            facts[g, r] = (
                [r % 2]
                + [r >> bit & 1 for bit in range(log_blocks)]
                + [g * shared, (1 - g) * kept]
                + [order[(place - d) % chips] if ringed else 0 for d in range(chips)]
            )
    k_mine, k_lacks, chip_at = 1 + log_blocks, 2 + log_blocks, 3 + log_blocks
    info = lax.dynamic_slice(jnp.asarray(facts), (group, rank, 0), (1, 1, facts.shape[2])).reshape(-1)

    def swap(block, bit, upward=False):
        route = [(r, r ^ 1 << bit) for r in range(devices) if not (upward and r >> bit & 1)]
        return lax.ppermute(block, "seq", route)

    other = (1 - core) * half
    w_got = swap(lax.dynamic_slice(out_weight, (other, 0), (half, columns)), 0)
    got = swap(
        jnp.concatenate(
            [lax.dynamic_slice(x, (0, other), (stretch, half)) for x in (keys, values, queries)], axis=0
        ),
        0,
    )
    index = jnp.concatenate([level_index, swap(level_index, 0)]).reshape(-1, 1)
    table = jnp.transpose(level_table, (2, 0, 1))

    w_own = lax.dynamic_slice(out_weight, (core * half, 0), (half, columns))
    whole = jnp.where(
        core == 0,
        jnp.concatenate([w_own, w_got], axis=1),
        jnp.concatenate([w_got, w_own], axis=1),
    )
    pieces = []
    plan = []
    if ringed:
        clockwise = []
        for at, chip in enumerate(order):
            follows = order[(at + 1) % chips]
            clockwise += [(2 * chip + c, 2 * follows + c) for c in range(2)]
        counter = [(b, a) for a, b in clockwise]
        pieces.append(whole)
        plan.append((chip_at, [(0, 0, None, 0, half)]))
        right = left = lax.dynamic_slice(whole, (group * shared, 0), (kept, 2 * columns)) if shared else whole
        rounds = chips // 2
        for r in range(1, rounds + 1):
            last = r == rounds
            if last:
                right, left = right[:cut], left[cut:]
            right = lax.ppermute(right, "seq", clockwise)
            left = lax.ppermute(left, "seq", counter)
            at = len(pieces)
            pieces += [right, left]
            if last:
                parts = [[(at, 0, k_mine, 0, cut), (at + 1, 0, k_mine, cut, kept - cut)]]
                distances = [r]
            else:
                parts = [[(at, 0, k_mine, 0, kept)], [(at + 1, 0, k_mine, 0, kept)]]
                distances = [r, chips - r]
            if shared:
                first = group * (kept - shared)
                if last:
                    wanted = lax.dynamic_slice(
                        jnp.concatenate([right, left], axis=0), (first, 0), (shared, 2 * columns)
                    )
                else:
                    wanted = jnp.concatenate(
                        [lax.dynamic_slice(x, (first, 0), (shared, 2 * columns)) for x in (right, left)], axis=0
                    )
                pieces.append(lax.ppermute(wanted, "grp", [(0, 1), (1, 0)]))
                for n, part in enumerate(parts):
                    part.append((at + 2, n * shared, k_lacks, 0, shared))
            plan += [(chip_at + d, part) for d, part in zip(distances, parts)]
    else:
        full = lax.all_gather(out_weight, "seq", axis=1, tiled=True)
        pieces.append(lax.dynamic_slice(full, (core * half, 0), (half, width)))
        plan.append((None, [(0, 0, None, 0, half)]))

    state = jax.ShapeDtypeStruct((pair_heads, head_dim, head_dim), jnp.float32)
    state16 = jax.ShapeDtypeStruct(state.shape, jnp.bfloat16)
    total, send, even = call(
        state_kernel,
        (state, state16, state16),
        [SM] + [VM] * 3,
        2 * stretch * width * head_dim,
        1 << 21,
        info, keys, values, got,
    )
    buckets = [even]
    for bit in range(1, log_blocks):
        came = swap(send, bit, upward=bit == log_blocks - 1)
        buckets.append(came)
        if bit + 1 < log_blocks:
            total = total + came
            send = total.astype(jnp.bfloat16)

    mixed = jax.ShapeDtypeStruct((2 * stretch, half), jnp.float32)
    acc = call(
        functools.partial(local_kernel, log_stretch),
        mixed,
        [SM] + [VM] * 7,
        8 * stretch * stretch * half,
        1 << 23,
        info, queries, keys, values, got, index, table, even,
    )
    early = list(range(1, log_blocks - 1))
    if early:
        acc = call(
            functools.partial(far_kernel, early, False, log_stretch),
            mixed,
            [SM] + [VM] * (5 + len(early)),
            4 * stretch * half * head_dim * len(early),
            1 << 23,
            info, queries, got, index, table, acc, *[buckets[b] for b in early],
        )
    normed = call(
        functools.partial(far_kernel, [log_blocks - 1], True, log_stretch),
        jax.ShapeDtypeStruct(mixed.shape, jnp.bfloat16),
        [SM] + [VM] * 7,
        4 * stretch * half * head_dim,
        1 << 23,
        info, queries, got, index, table, acc, buckets[-1], norm_gain.reshape(1, width),
    )

    def project(side, dtype):
        return call(
            functools.partial(project_kernel, side, plan),
            jax.ShapeDtypeStruct((stretch, width), dtype),
            [SM] + [VM] * (1 + len(pieces)),
            2 * stretch * half * width,
            1 << 23,
            info, normed, *pieces,
        )

    came = swap(project(1, jnp.bfloat16), 0)
    return (project(0, jnp.float32) + came).astype(jnp.bfloat16)


def solution(mesh):
    placed = (
        P(("grp", "seq"), None),
        P(("grp", "seq"), None),
        P(("grp", "seq"), None),
        P(("grp", "seq")),
        P(),
        P(),
        P(None, "seq"),
    )
    return jax.shard_map(
        functools.partial(body, mesh.shape["grp"]),
        mesh=mesh,
        in_specs=placed,
        out_specs=P(("grp", "seq"), None),
        check_vma=False,
    )
```

```python
import functools
import math

import numpy as np

import jax
import jax.numpy as jnp
from jax import lax
from jax.experimental import pallas as pl
from jax.experimental.pallas import tpu as pltpu
from jax.sharding import PartitionSpec as P

TILE = 128
VM = pl.BlockSpec(memory_space=pltpu.VMEM)
SM = pl.BlockSpec(memory_space=pltpu.SMEM)
PARAMS = pltpu.CompilerParams(vmem_limit_bytes=8 * 1024 * 1024)


def call(kernel, out_shape, in_specs, flops, moved, *operands):
    outs = jax.tree.map(lambda _: VM, out_shape)
    return pl.pallas_call(
        kernel,
        out_shape=out_shape,
        in_specs=in_specs,
        out_specs=outs,
        compiler_params=PARAMS,
        cost_estimate=pl.CostEstimate(flops=flops, bytes_accessed=moved, transcendentals=0),
    )(*operands)


def us(microseconds):
    return int(microseconds * 1.15e9)


def lanes(start, size):
    return pl.ds(pl.multiple_of(start, TILE), size)


def dot(a, b, ca=1, cb=0):
    return lax.dot_general(a, b, (((ca,), (cb,)), ((), ())), preferred_element_type=jnp.float32)


def split_kernel(k_ref, v_ref, q_ref, w_ref, index_ref, sent_ref, mine_ref, w_sent_ref, w_mine_ref, sems):
    rows, half = mine_ref.shape[0] // 3, mine_ref.shape[1]
    deep = w_mine_ref.shape[0]
    core = lax.axis_index("seq") % 2
    copies = []
    for to_other, big, small in ((1, sent_ref, w_sent_ref), (0, mine_ref, w_mine_ref)):
        side = (core + to_other) % 2
        for at, ref in enumerate((k_ref, v_ref, q_ref)):
            copies.append((ref.at[:, lanes(side * half, half)], big.at[pl.ds(at * rows, rows), :]))
        copies.append((w_ref.at[pl.ds(pl.multiple_of(side * deep, 16), deep), :], small))
    copies = [pltpu.make_async_copy(a, b, sems.at[n]) for n, (a, b) in enumerate(copies)]
    for copy in copies:
        copy.start()
    if sent_ref.shape[0] > 3 * rows:
        tail = sent_ref.shape[0] - 3 * rows
        row = jnp.broadcast_to(index_ref[...].astype(jnp.float32), (tail, rows)).astype(jnp.bfloat16)
        sent_ref[pl.ds(3 * rows, tail), :] = jnp.zeros((tail, half), jnp.bfloat16)
        sent_ref[pl.ds(3 * rows, tail), pl.ds(0, rows)] = row
    for copy in copies:
        copy.wait()


def state_kernel(info, mine_ref, got_ref, sum_ref, send_ref, even_ref):
    heads, dim, _ = sum_ref.shape
    rows = mine_ref.shape[0] // 3
    core = info[0]
    for h in range(heads):
        far = pl.ds(h * dim, dim)
        mine = dot(mine_ref[pl.ds(rows, rows), far], mine_ref[pl.ds(0, rows), far], 0, 0)
        theirs = dot(got_ref[pl.ds(rows, rows), far], got_ref[pl.ds(0, rows), far], 0, 0)
        both = mine + theirs
        sum_ref[h] = both
        send_ref[h] = both.astype(jnp.bfloat16)
        even_ref[h] = jnp.where(core == 0, mine, theirs).astype(jnp.bfloat16)


def local_kernel(lam_ref, part_ref, out_ref):
    heads = lam_ref.shape[0]
    dim, rows = out_ref.shape[0] // heads, out_ref.shape[1]
    scale = 1.0 / math.sqrt(dim)
    step = min(TILE, rows)
    blocks = rows // step
    log_step = step.bit_length() - 1
    s_at = lax.broadcasted_iota(jnp.int32, (step, step), 0)
    t_at = lax.broadcasted_iota(jnp.int32, (step, step), 1)
    grid = jnp.zeros((step, step), jnp.int32)
    for bit in range(log_step):
        grid = grid + (jnp.right_shift(t_at, bit) != jnp.right_shift(s_at, bit)).astype(jnp.int32)
    grid = jnp.where(s_at <= t_at, grid, -1)
    for h in range(heads):

        def part(which, first, count):
            return part_ref[pl.ds(which * rows + first, count), pl.ds(h * dim, dim)]

        lam = lam_ref[h] * scale
        totals = [None] * blocks
        for s in range(blocks):
            scores = dot(part(0, s * step, step), part(2, s * step, rows - s * step), 1, 1)
            weighted = []
            for t in range(s, blocks):
                lam_t = lam[:, t * step : (t + 1) * step]
                if s == t:
                    picked = jnp.zeros((step, step), jnp.float32)
                    for level in range(log_step + 1):
                        picked = jnp.where(grid == level, lam_t[level : level + 1], picked)
                else:
                    level = log_step + (s ^ t).bit_length()
                    picked = lam_t[level : level + 1]
                weighted.append((picked * scores[:, (t - s) * step : (t - s + 1) * step]).astype(jnp.bfloat16))
            joined = weighted[0] if len(weighted) == 1 else jnp.concatenate(weighted, axis=1)
            add = dot(part(1, s * step, step), joined, 0, 0)
            for t in range(s, blocks):
                term = add[:, (t - s) * step : (t - s + 1) * step]
                totals[t] = term if totals[t] is None else totals[t] + term
        for t in range(blocks):
            out_ref[pl.ds(h * dim, dim), pl.ds(t * step, step)] = totals[t]


def early_kernel(levels, log_stretch, info, mine_ref, got_ref, lam0_ref, lam1_ref, base0_ref, base1_ref, *refs):
    buckets, out_ref = refs[:-1], refs[-1]
    heads = lam0_ref.shape[0]
    rows = mine_ref.shape[0] // 3
    dim = base0_ref.shape[0] // heads
    core = info[0]
    scale = 1.0 / math.sqrt(dim)
    for h in range(heads):
        far = pl.ds(h * dim, dim)
        for side in range(2):
            odd = core if side == 0 else 1 - core
            lam = (lam0_ref, lam1_ref)[side][h]
            q = (mine_ref, got_ref)[side][pl.ds(2 * rows, rows), far]
            total = (base0_ref, base1_ref)[side][far, :]
            for at, level in enumerate(levels):
                column = log_stretch + 1 + level
                on = odd if level == 0 else info[1 + level]
                weight = jnp.where(on == 1, lam[column : column + 1] * scale, 0.0)
                total = total + weight * dot(buckets[at][h], q, 1, 1)
            out_ref[far, pl.ds(side * rows, rows)] = total


def last_kernel(level, log_stretch, info, mine_ref, got_ref, lam0_ref, lam1_ref, base_ref, bucket_ref, gain_ref, out_ref):
    heads = lam0_ref.shape[0]
    rows = mine_ref.shape[0] // 3
    dim = base_ref.shape[0] // heads
    core = info[0]
    scale = 1.0 / math.sqrt(dim)
    column = log_stretch + 1 + level
    for h in range(heads):
        far = pl.ds(h * dim, dim)
        own = lanes(core * heads * dim + h * dim, dim)
        for side in range(2):
            at_rows = pl.ds(side * rows, rows)
            lam = (lam0_ref, lam1_ref)[side][h]
            q = (mine_ref, got_ref)[side][pl.ds(2 * rows, rows), far]
            weight = jnp.where(info[1 + level] == 1, lam[column : column + 1] * scale, 0.0)
            total = base_ref[far, at_rows] + weight * dot(bucket_ref[h], q, 1, 1)
            mean = jnp.mean(total * total, axis=0, keepdims=True)
            total = total * lax.rsqrt(mean + 1e-06)
            out_ref[at_rows, far] = (jnp.transpose(total) * gain_ref[:, own]).astype(out_ref.dtype)


def project_kernel(side, plan, info, normed_ref, *refs):
    out_ref = refs[-1]
    rows = out_ref.shape[0]
    for chip_slot, parts in plan:
        total = None
        for at, row0, k_slot, k_add, size in parts:
            piece = refs[at]
            start = k_add if k_slot is None else info[k_slot] + k_add
            a = normed_ref[pl.ds(side * rows, rows), lanes(start, size)]
            term = dot(a, piece[pl.ds(row0, size), :])
            total = term if total is None else total + term
        width = refs[parts[0][0]].shape[1]
        column = 0 if chip_slot is None else info[chip_slot] * width
        out_ref[:, lanes(column, width)] = total.astype(out_ref.dtype)


def ring_order(chips):
    return list(range(0, chips, 2)) + list(range(chips - 1, 0, -2))


def body(groups, queries, keys, values, level_index, level_table, norm_gain, out_weight):
    stretch, width = queries.shape
    table_rows, level_count, heads = level_table.shape
    head_dim = width // heads
    columns = out_weight.shape[1]
    log_stretch = stretch.bit_length() - 1
    devices = lax.axis_size("seq")
    log_blocks = devices.bit_length() - 1
    rank = lax.axis_index("seq")
    group = lax.axis_index("grp")
    core = rank % 2
    half = width // 2
    pair_heads = heads // 2
    chips = devices // 2
    ringed = (2 * columns) % TILE == 0 and chips >= 4
    shared = (3 * half // 8) // TILE * TILE if ringed and groups == 2 else 0
    kept = half - shared
    cut = kept // TILE // 2 * TILE

    order = ring_order(chips)
    facts = np.zeros((groups, devices, 1 + log_blocks + 2 + chips), np.int32)
    for g in range(groups):
        for r in range(devices):
            place = order.index(r // 2) if ringed else 0
            facts[g, r] = (
                [r % 2]
                + [r >> bit & 1 for bit in range(log_blocks)]
                + [g * shared, (1 - g) * kept]
                + [order[(place - d) % chips] if ringed else 0 for d in range(chips)]
            )
    k_mine, k_lacks, chip_at = 1 + log_blocks, 2 + log_blocks, 3 + log_blocks
    info = lax.dynamic_slice(jnp.asarray(facts), (group, rank, 0), (1, 1, facts.shape[2])).reshape(-1)

    def swap(block, bit, upward=False):
        route = [(r, r ^ 1 << bit) for r in range(devices) if not (upward and r >> bit & 1)]
        return lax.ppermute(block, "seq", route)

    packs = table_rows <= 256 and stretch <= half
    bf16 = functools.partial(jax.ShapeDtypeStruct, dtype=jnp.bfloat16)
    sent, mine, w_sent, w_own = pl.pallas_call(
        split_kernel,
        out_shape=(
            bf16(((3 * stretch + 16) if packs else 3 * stretch, half)),
            bf16((3 * stretch, half)),
            bf16((half, columns)),
            bf16((half, columns)),
        ),
        in_specs=[pl.BlockSpec(memory_space=pltpu.HBM)] * 4 + [VM],
        out_specs=(VM,) * 4,
        scratch_shapes=[pltpu.SemaphoreType.DMA((8,))],
        compiler_params=pltpu.CompilerParams(vmem_limit_bytes=56 * 1024 * 1024),
        cost_estimate=pl.CostEstimate(flops=us(1.5), bytes_accessed=1 << 21, transcendentals=0),
    )(keys, values, queries, out_weight, level_index.reshape(1, stretch))
    got = swap(sent, 0)
    if packs:
        index_got = got[3 * stretch, :stretch].astype(jnp.int32)
    else:
        index_got = swap(level_index, 0)

    w_got = swap(w_sent, 0)
    whole = jnp.where(
        core == 0,
        jnp.concatenate([w_own, w_got], axis=1),
        jnp.concatenate([w_got, w_own], axis=1),
    )

    table = jnp.transpose(level_table, (2, 1, 0))
    table = jnp.where(core == 0, table[:pair_heads], table[pair_heads:]).reshape(-1, table_rows)

    def level_weights(index):
        found = (index[None, :] == jnp.arange(table_rows, dtype=jnp.int32)[:, None]).astype(jnp.float32)
        lam = jnp.dot(table, found, precision=lax.Precision.HIGHEST)
        return lam.reshape(pair_heads, level_count, stretch)

    lam_own = level_weights(level_index)
    lam_got = level_weights(index_got)

    state = jax.ShapeDtypeStruct((pair_heads, head_dim, head_dim), jnp.float32)
    state16 = jax.ShapeDtypeStruct(state.shape, jnp.bfloat16)
    total, send, even = call(
        state_kernel,
        (state, state16, state16),
        [SM] + [VM] * 2,
        us(1.0),
        1 << 20,
        info, mine, got,
    )
    buckets = [even]
    reached = [send]
    upper = jnp.right_shift(rank, 1) % 2
    for bit in range(1, log_blocks):
        came = swap(send, bit, upward=bit == log_blocks - 1)
        if bit + 1 < log_blocks:
            total = total + came
            if bit == 1:
                total = jnp.where(upper == 0, total[: pair_heads // 2], total[pair_heads // 2 :])
            send = total.astype(jnp.bfloat16)
            reached.append(send)
        if bit > 1:
            rest = swap(came, 1)
            came = jnp.where(
                upper == 0, jnp.concatenate([came, rest], axis=0), jnp.concatenate([rest, came], axis=0)
            )
        buckets.append(came)

    pieces = []
    plan = []
    crossed = []
    if ringed:
        clockwise = []
        for at, chip in enumerate(order):
            follows = order[(at + 1) % chips]
            clockwise += [(2 * chip + c, 2 * follows + c) for c in range(2)]
        counter = [(b, a) for a, b in clockwise]
        pieces.append(whole)
        plan.append((chip_at, [(0, 0, None, 0, half)]))
        right = left = jnp.where(group % 2 == 0, whole[:kept], whole[shared:]) if shared else whole
        rounds = chips // 2
        for r in range(1, rounds + 1):
            last = r == rounds
            ahead = reached[r - 1 : r] + crossed[r - 3 : r - 2] * (r >= 3)
            right, left, *_ = lax.optimization_barrier((right, left, *ahead))
            if last:
                right, left = right[:cut], left[cut:]
            right = lax.ppermute(right, "seq", clockwise)
            left = lax.ppermute(left, "seq", counter)
            at = len(pieces)
            pieces += [right, left]
            if last:
                parts = [[(at, 0, k_mine, 0, cut), (at + 1, 0, k_mine, cut, kept - cut)]]
                distances = [r]
            else:
                parts = [[(at, 0, k_mine, 0, kept)], [(at + 1, 0, k_mine, 0, kept)]]
                distances = [r, chips - r]
            if shared:
                held = [jnp.concatenate([right, left], axis=0)] if last else [right, left]
                low, high = ([x[at:][:shared] for x in held] for at in (0, kept - shared))
                wanted = jnp.where(group == 0, jnp.concatenate(low, axis=0), jnp.concatenate(high, axis=0))
                crossed.append(lax.ppermute(wanted, "grp", [(0, 1), (1, 0)]))
                pieces.append(crossed[-1])
                for n, part in enumerate(parts):
                    part.append((at + 2, n * shared, k_lacks, 0, shared))
            plan += [(chip_at + d, part) for d, part in zip(distances, parts)]
    else:
        full = lax.all_gather(out_weight, "seq", axis=1, tiled=True)
        pieces.append(lax.dynamic_slice(full, (core * half, 0), (half, width)))
        plan.append((None, [(0, 0, None, 0, half)]))

    side_shape = jax.ShapeDtypeStruct((half, stretch), jnp.float32)
    acc_own = call(
        local_kernel, side_shape, [VM] * 2, us(2.9), 1 << 21, lam_own, mine,
    )
    acc_got = call(
        local_kernel, side_shape, [VM] * 2, us(2.9), 1 << 21, lam_got, got,
    )
    early = list(range(log_blocks - 1))
    acc = call(
        functools.partial(early_kernel, early, log_stretch),
        jax.ShapeDtypeStruct((half, 2 * stretch), jnp.float32),
        [SM] + [VM] * (6 + len(early)),
        us(3.5),
        1 << 21,
        info, mine, got, lam_own, lam_got, acc_own, acc_got, *buckets[:-1],
    )
    normed = call(
        functools.partial(last_kernel, log_blocks - 1, log_stretch),
        jax.ShapeDtypeStruct((2 * stretch, half), jnp.bfloat16),
        [SM] + [VM] * 7,
        us(2.5),
        1 << 21,
        info, mine, got, lam_own, lam_got, acc, buckets[-1], norm_gain.reshape(1, width),
    )

    def project(side, dtype):
        return call(
            functools.partial(project_kernel, side, plan),
            jax.ShapeDtypeStruct((stretch, width), dtype),
            [SM] + [VM] * (1 + len(pieces)),
            us(3.0),
            1 << 21,
            info, normed, *pieces,
        )

    came = swap(project(1, jnp.bfloat16), 0)
    return (project(0, jnp.float32) + came).astype(jnp.bfloat16)


def solution(mesh):
    placed = (
        P(("grp", "seq"), None),
        P(("grp", "seq"), None),
        P(("grp", "seq"), None),
        P(("grp", "seq")),
        P(),
        P(),
        P(None, "seq"),
    )
    return jax.shard_map(
        functools.partial(body, mesh.shape["grp"]),
        mesh=mesh,
        in_specs=placed,
        out_specs=P(("grp", "seq"), None),
        check_vma=False,
    )
```

```python
import functools
import math

import numpy as np

import jax
import jax.numpy as jnp
from jax import lax
from jax.experimental import pallas as pl
from jax.experimental.pallas import tpu as pltpu
from jax.sharding import PartitionSpec as P

TILE = 128
LATE = 1
VM = pl.BlockSpec(memory_space=pltpu.VMEM)
SM = pl.BlockSpec(memory_space=pltpu.SMEM)
PARAMS = pltpu.CompilerParams(vmem_limit_bytes=8 * 1024 * 1024)


def call(kernel, out_shape, in_specs, flops, moved, *operands):
    outs = jax.tree.map(lambda _: VM, out_shape)
    return pl.pallas_call(
        kernel,
        out_shape=out_shape,
        in_specs=in_specs,
        out_specs=outs,
        compiler_params=PARAMS,
        cost_estimate=pl.CostEstimate(flops=flops, bytes_accessed=moved, transcendentals=0),
    )(*operands)


def us(microseconds):
    return int(microseconds * 1.15e9)


def lanes(start, size):
    return pl.ds(pl.multiple_of(start, TILE), size)


def dot(a, b, ca=1, cb=0):
    return lax.dot_general(a, b, (((ca,), (cb,)), ((), ())), preferred_element_type=jnp.float32)


def split_kernel(to_other, k_ref, v_ref, q_ref, index_ref, after_ref, out_ref, sems):
    half = out_ref.shape[1]
    rows = k_ref.shape[0]
    side = (lax.axis_index("seq") + to_other) % 2
    copies = []
    for at, ref in enumerate((k_ref, v_ref, q_ref)):
        copies.append((ref.at[:, lanes(side * half, half)], out_ref.at[pl.ds(at * rows, rows), :]))
    copies = [pltpu.make_async_copy(a, b, sems.at[n]) for n, (a, b) in enumerate(copies)]
    for copy in copies:
        copy.start()
    tail = out_ref.shape[0] - 3 * rows
    if tail:
        row = jnp.broadcast_to(index_ref[...].astype(jnp.float32), (tail, rows)).astype(jnp.bfloat16)
        out_ref[pl.ds(3 * rows, tail), :] = jnp.zeros((tail, half), jnp.bfloat16)
        out_ref[pl.ds(3 * rows, tail), pl.ds(0, rows)] = row
    for copy in copies:
        copy.wait()


def state_kernel(info, mine_ref, got_ref, sum_ref, send_ref, even_ref):
    heads, dim, _ = sum_ref.shape
    rows = mine_ref.shape[0] // 3
    core = info[0]
    for h in range(heads):
        far = pl.ds(h * dim, dim)
        mine = dot(mine_ref[pl.ds(rows, rows), far], mine_ref[pl.ds(0, rows), far], 0, 0)
        theirs = dot(got_ref[pl.ds(rows, rows), far], got_ref[pl.ds(0, rows), far], 0, 0)
        both = mine + theirs
        sum_ref[h] = both
        send_ref[h] = both.astype(jnp.bfloat16)
        even_ref[h] = jnp.where(core == 0, mine, theirs).astype(jnp.bfloat16)


def local_kernel(lam_ref, part_ref, out_ref):
    heads = lam_ref.shape[0]
    dim, rows = out_ref.shape[0] // heads, out_ref.shape[1]
    scale = 1.0 / math.sqrt(dim)
    step = min(TILE, rows)
    blocks = rows // step
    log_step = step.bit_length() - 1
    s_at = lax.broadcasted_iota(jnp.int32, (step, step), 0)
    t_at = lax.broadcasted_iota(jnp.int32, (step, step), 1)
    grid = jnp.zeros((step, step), jnp.int32)
    for bit in range(log_step):
        grid = grid + (jnp.right_shift(t_at, bit) != jnp.right_shift(s_at, bit)).astype(jnp.int32)
    grid = jnp.where(s_at <= t_at, grid, -1)
    for h in range(heads):

        def part(which, first, count):
            return part_ref[pl.ds(which * rows + first, count), pl.ds(h * dim, dim)]

        lam = lam_ref[h] * scale
        totals = [None] * blocks
        for s in range(blocks):
            scores = dot(part(0, s * step, step), part(2, s * step, rows - s * step), 1, 1)
            weighted = []
            for t in range(s, blocks):
                lam_t = lam[:, t * step : (t + 1) * step]
                if s == t:
                    picked = jnp.zeros((step, step), jnp.float32)
                    for level in range(log_step + 1):
                        picked = jnp.where(grid == level, lam_t[level : level + 1], picked)
                else:
                    level = log_step + (s ^ t).bit_length()
                    picked = lam_t[level : level + 1]
                weighted.append((picked * scores[:, (t - s) * step : (t - s + 1) * step]).astype(jnp.bfloat16))
            joined = weighted[0] if len(weighted) == 1 else jnp.concatenate(weighted, axis=1)
            add = dot(part(1, s * step, step), joined, 0, 0)
            for t in range(s, blocks):
                term = add[:, (t - s) * step : (t - s + 1) * step]
                totals[t] = term if totals[t] is None else totals[t] + term
        for t in range(blocks):
            out_ref[pl.ds(h * dim, dim), pl.ds(t * step, step)] = totals[t]


def early_kernel(levels, log_stretch, info, mine_ref, got_ref, lam0_ref, lam1_ref, base0_ref, base1_ref, *refs):
    buckets, out_ref = refs[:-1], refs[-1]
    heads = lam0_ref.shape[0]
    rows = mine_ref.shape[0] // 3
    dim = base0_ref.shape[0] // heads
    core = info[0]
    scale = 1.0 / math.sqrt(dim)
    for h in range(heads):
        far = pl.ds(h * dim, dim)
        for side in range(2):
            odd = core if side == 0 else 1 - core
            lam = (lam0_ref, lam1_ref)[side][h]
            q = (mine_ref, got_ref)[side][pl.ds(2 * rows, rows), far]
            total = (base0_ref, base1_ref)[side][far, :]
            for at, level in enumerate(levels):
                column = log_stretch + 1 + level
                on = odd if level == 0 else info[1 + level]
                weight = jnp.where(on == 1, lam[column : column + 1] * scale, 0.0)
                total = total + weight * dot(buckets[at][h], q, 1, 1)
            out_ref[far, pl.ds(side * rows, rows)] = total


def last_kernel(levels, log_stretch, info, mine_ref, got_ref, lam0_ref, lam1_ref, base_ref, gain_ref, *refs):
    buckets, out_ref = refs[:-1], refs[-1]
    heads = lam0_ref.shape[0]
    rows = mine_ref.shape[0] // 3
    dim = base_ref.shape[0] // heads
    core = info[0]
    scale = 1.0 / math.sqrt(dim)
    for h in range(heads):
        far = pl.ds(h * dim, dim)
        own = lanes(core * heads * dim + h * dim, dim)
        for side in range(2):
            at_rows = pl.ds(side * rows, rows)
            lam = (lam0_ref, lam1_ref)[side][h]
            q = (mine_ref, got_ref)[side][pl.ds(2 * rows, rows), far]
            total = base_ref[far, at_rows]
            for at, level in enumerate(levels):
                column = log_stretch + 1 + level
                weight = jnp.where(info[1 + level] == 1, lam[column : column + 1] * scale, 0.0)
                total = total + weight * dot(buckets[at][h], q, 1, 1)
            mean = jnp.mean(total * total, axis=0, keepdims=True)
            total = total * lax.rsqrt(mean + 1e-06)
            out_ref[at_rows, far] = (jnp.transpose(total) * gain_ref[:, own]).astype(out_ref.dtype)


def project_kernel(plan, info, normed_ref, *refs):
    pieces, own_ref, other_ref = refs[:-2], refs[-2], refs[-1]
    rows = own_ref.shape[0]
    for slot, (_, parts) in enumerate(plan):
        total = None
        for at, row0, k_slot, k_add, size in parts:
            start = k_add if k_slot is None else info[k_slot] + k_add
            term = dot(normed_ref[:, lanes(start, size)], pieces[at][pl.ds(row0, size), :])
            total = term if total is None else total + term
        width = pieces[parts[0][0]].shape[1]
        own_ref[:, pl.ds(slot * width, width)] = total[:rows]
        other_ref[:, pl.ds(slot * width, width)] = total[rows:].astype(other_ref.dtype)


def combine_kernel(plans, info, *refs):
    out_ref, held, sems = refs[-3:]
    copies = []
    for n, plan in enumerate(plans):
        own_ref, came_ref = refs[2 * n], refs[2 * n + 1]
        width = own_ref.shape[1] // len(plan)
        for slot, (chip_slot, _) in enumerate(plan):
            at = pl.ds(slot * width, width)
            column = 0 if chip_slot is None else info[chip_slot] * width
            total = own_ref[:, at] + came_ref[:, at].astype(jnp.float32)
            to = pl.ds(len(copies) * width, width)
            held[:, to] = total.astype(out_ref.dtype)
            copy = pltpu.make_async_copy(held.at[:, to], out_ref.at[:, lanes(column, width)], sems.at[len(copies)])
            copy.start()
            copies.append(copy)
    for copy in copies:
        copy.wait()


def ring_order(chips):
    return list(range(0, chips, 2)) + list(range(chips - 1, 0, -2))


def body(groups, queries, keys, values, level_index, level_table, norm_gain, out_weight):
    stretch, width = queries.shape
    table_rows, level_count, heads = level_table.shape
    head_dim = width // heads
    columns = out_weight.shape[1]
    log_stretch = stretch.bit_length() - 1
    devices = lax.axis_size("seq")
    log_blocks = devices.bit_length() - 1
    rank = lax.axis_index("seq")
    group = lax.axis_index("grp")
    core = rank % 2
    half = width // 2
    pair_heads = heads // 2
    chips = devices // 2
    ringed = (2 * columns) % TILE == 0 and chips >= 4
    shared = (3 * half // 8) // TILE * TILE if ringed and groups == 2 else 0
    kept = half - shared
    cut = kept // TILE // 2 * TILE

    order = ring_order(chips)
    facts = np.zeros((groups, devices, 1 + log_blocks + 2 + chips), np.int32)
    for g in range(groups):
        for r in range(devices):
            place = order.index(r // 2) if ringed else 0
            facts[g, r] = (
                [r % 2]
                + [r >> bit & 1 for bit in range(log_blocks)]
                + [g * shared, (1 - g) * kept]
                + [order[(place - d) % chips] if ringed else 0 for d in range(chips)]
            )
    k_mine, k_lacks, chip_at = 1 + log_blocks, 2 + log_blocks, 3 + log_blocks
    info = lax.dynamic_slice(jnp.asarray(facts), (group, rank, 0), (1, 1, facts.shape[2])).reshape(-1)

    def swap(block, bit, upward=False):
        route = [(r, r ^ 1 << bit) for r in range(devices) if not (upward and r >> bit & 1)]
        return lax.ppermute(block, "seq", route)

    packs = table_rows <= 256 and stretch <= half
    bf16 = functools.partial(jax.ShapeDtypeStruct, dtype=jnp.bfloat16)

    def split(to_other, rows, after):
        hbm = pl.BlockSpec(memory_space=pltpu.HBM)
        return pl.pallas_call(
            functools.partial(split_kernel, to_other),
            out_shape=bf16((rows, half)),
            in_specs=[hbm] * 3 + [VM, pl.BlockSpec(memory_space=pl.ANY)],
            out_specs=VM,
            scratch_shapes=[pltpu.SemaphoreType.DMA((3,))],
            compiler_params=pltpu.CompilerParams(vmem_limit_bytes=56 * 1024 * 1024),
            cost_estimate=pl.CostEstimate(flops=us(2.5), bytes_accessed=1 << 21, transcendentals=0),
        )(keys, values, queries, level_index.reshape(1, stretch), after)

    w_got = swap(out_weight, 0)
    sent = split(1, (3 * stretch + 16) if packs else 3 * stretch, level_index)
    got = swap(sent, 0)
    if packs:
        index_got = got[3 * stretch, :stretch].astype(jnp.int32)
    else:
        index_got = swap(level_index, 0)

    whole = jnp.where(
        core == 0,
        jnp.concatenate([out_weight[:half], w_got[:half]], axis=1),
        jnp.concatenate([w_got[half:], out_weight[half:]], axis=1),
    )

    mine = split(0, 3 * stretch, whole)
    table = jnp.transpose(level_table, (2, 1, 0))
    table = jnp.where(core == 0, table[:pair_heads], table[pair_heads:]).reshape(-1, table_rows)

    def level_weights(index):
        found = (index[None, :] == jnp.arange(table_rows, dtype=jnp.int32)[:, None]).astype(jnp.float32)
        lam = jnp.dot(table, found, precision=lax.Precision.HIGHEST)
        return lam.reshape(pair_heads, level_count, stretch)

    lam_own = level_weights(level_index)
    lam_got = level_weights(index_got)

    state = jax.ShapeDtypeStruct((pair_heads, head_dim, head_dim), jnp.float32)
    state16 = jax.ShapeDtypeStruct(state.shape, jnp.bfloat16)
    total, send, even = call(
        state_kernel,
        (state, state16, state16),
        [SM] + [VM] * 2,
        us(1.0),
        1 << 20,
        info, mine, got,
    )
    send_first = send
    buckets = [even]
    quarters = []
    reached = [send]
    upper = jnp.right_shift(rank, 1) % 2
    crossed = []

    def tie(x, *others):
        return lax.optimization_barrier((x, *others))[0]

    def level(bit):
        nonlocal total, send
        came = swap(send, bit, upward=bit == log_blocks - 1)
        if bit + 1 < log_blocks:
            total = total + came
            if bit == 1:
                total = jnp.where(upper == 0, total[: pair_heads // 2], total[pair_heads // 2 :])
            send = total.astype(jnp.bfloat16)
            reached.append(send)
        if bit > 1:
            quarters.append(came)
        else:
            buckets.append(came)

    for bit in range(1, min(3, log_blocks)):
        level(bit)

    pieces = []
    plan = []
    late = []
    landed = ()
    if ringed:
        clockwise = []
        for at, chip in enumerate(order):
            follows = order[(at + 1) % chips]
            clockwise += [(2 * chip + c, 2 * follows + c) for c in range(2)]
        counter = [(b, a) for a, b in clockwise]
        pieces.append(whole)
        plan.append((chip_at, [(0, 0, None, 0, half)]))
        right = left = jnp.where(group % 2 == 0, whole[:kept], whole[shared:]) if shared else whole
        rounds = chips // 2

        def ring_after(r):
            if r == 3:
                return reached[2:3] + crossed[:1]
            return []

        for r in range(1, rounds + 1):
            last = r == rounds
            right, left, *_ = lax.optimization_barrier((right, left, *ring_after(r)))
            if last:
                right, left = right[:cut], left[cut:]
            right = lax.ppermute(right, "seq", clockwise)
            left = lax.ppermute(left, "seq", counter)
            if r == 1:
                right, left, _ = lax.optimization_barrier((right, left, send_first))
            if r == 3:
                send = tie(send, right, left)
            at = len(pieces)
            pieces += [right, left]
            landed = (right, left)
            if last:
                parts = [[(at, 0, k_mine, 0, cut), (at + 1, 0, k_mine, cut, kept - cut)]]
                distances = [r]
            else:
                parts = [[(at, 0, k_mine, 0, kept)], [(at + 1, 0, k_mine, 0, kept)]]
                distances = [r, chips - r]
            if shared:
                held = [jnp.concatenate([right, left], axis=0)] if last else [right, left]
                low, high = ([x[at:][:shared] for x in held] for at in (0, kept - shared))
                wanted = jnp.where(group == 0, jnp.concatenate(low, axis=0), jnp.concatenate(high, axis=0))
                crossed.append(lax.ppermute(wanted, "grp", [(0, 1), (1, 0)]))
                pieces.append(crossed[-1])
                for n, part in enumerate(parts):
                    part.append((at + 2, n * shared, k_lacks, 0, shared))
            (late if r >= rounds - LATE else plan).extend(
                (chip_at + d, part) for d, part in zip(distances, parts)
            )
    else:
        full = lax.all_gather(out_weight, "seq", axis=1, tiled=True)
        pieces.append(lax.dynamic_slice(full, (core * half, 0), (half, width)))
        plan.append((None, [(0, 0, None, 0, half)]))

    while len(quarters) + 2 < log_blocks:
        level(len(quarters) + 2)
    joined = jnp.stack(quarters)
    rest = swap(joined, 1)
    both = jnp.where(
        upper == 0, jnp.concatenate([joined, rest], axis=1), jnp.concatenate([rest, joined], axis=1)
    )
    buckets += [both[n] for n in range(len(quarters))]

    side_shape = jax.ShapeDtypeStruct((half, stretch), jnp.float32)
    acc_own = call(
        local_kernel, side_shape, [VM] * 2, us(2.1), 1 << 20, tie(lam_own, reached[0]), mine,
    )
    acc_got = call(
        local_kernel, side_shape, [VM] * 2, us(2.1), 1 << 20, lam_got, got,
    )
    acc = call(
        functools.partial(early_kernel, [0, 1], log_stretch),
        jax.ShapeDtypeStruct((half, 2 * stretch), jnp.float32),
        [SM] + [VM] * 8,
        us(1.6),
        1 << 20,
        info, mine, got, lam_own, lam_got, acc_own, acc_got, *buckets[:2],
    )
    normed = call(
        functools.partial(last_kernel, list(range(2, log_blocks)), log_stretch),
        jax.ShapeDtypeStruct((2 * stretch, half), jnp.bfloat16),
        [SM] + [VM] * (6 + len(quarters)),
        us(2.0),
        1 << 20,
        info, mine, got, lam_own, lam_got, acc, norm_gain.reshape(1, width), *buckets[2:],
    )

    plans = [p for p in (plan, late) if p]
    shares = []
    for p in plans:
        used = sorted({part[0] for _, parts in p for part in parts})
        local = [(c, [(used.index(part[0]), *part[1:]) for part in parts]) for c, parts in p]
        wide = len(p) * pieces[used[0]].shape[1]
        own, other = call(
            functools.partial(project_kernel, local),
            (
                jax.ShapeDtypeStruct((stretch, wide), jnp.float32),
                jax.ShapeDtypeStruct((stretch, wide), jnp.bfloat16),
            ),
            [SM] + [VM] * (1 + len(used)),
            us(4.0 * wide / width),
            1 << 20,
            info, normed, *[pieces[n] for n in used],
        )
        shares += [own, swap(other, 0)]
    return pl.pallas_call(
        functools.partial(combine_kernel, plans),
        out_shape=jax.ShapeDtypeStruct((stretch, width), jnp.bfloat16),
        in_specs=[SM] + [VM] * len(shares),
        out_specs=pl.BlockSpec(memory_space=pltpu.HBM),
        scratch_shapes=[
            pltpu.VMEM((stretch, width), jnp.bfloat16),
            pltpu.SemaphoreType.DMA((sum(len(p) for p in plans),)),
        ],
        compiler_params=PARAMS,
        cost_estimate=pl.CostEstimate(flops=us(1.0), bytes_accessed=1 << 20, transcendentals=0),
    )(info, *shares)


def solution(mesh):
    placed = (
        P(("grp", "seq"), None),
        P(("grp", "seq"), None),
        P(("grp", "seq"), None),
        P(("grp", "seq")),
        P(),
        P(),
        P(None, "seq"),
    )
    return jax.shard_map(
        functools.partial(body, mesh.shape["grp"]),
        mesh=mesh,
        in_specs=placed,
        out_specs=P(("grp", "seq"), None),
        check_vma=False,
    )
```

```python
import functools
import math

import numpy as np

import jax
import jax.numpy as jnp
from jax import lax
from jax.experimental import pallas as pl
from jax.experimental.pallas import tpu as pltpu
from jax.sharding import PartitionSpec as P

TILE = 128
VM = pl.BlockSpec(memory_space=pltpu.VMEM)
SM = pl.BlockSpec(memory_space=pltpu.SMEM)
PARAMS = pltpu.CompilerParams(vmem_limit_bytes=8 * 1024 * 1024)


def call(kernel, out_shape, in_specs, flops, moved, *operands):
    outs = jax.tree.map(lambda _: VM, out_shape)
    return pl.pallas_call(
        kernel,
        out_shape=out_shape,
        in_specs=in_specs,
        out_specs=outs,
        compiler_params=PARAMS,
        cost_estimate=pl.CostEstimate(flops=flops, bytes_accessed=moved, transcendentals=0),
    )(*operands)


def us(microseconds):
    return int(microseconds * 1.15e9)


def lanes(start, size):
    return pl.ds(pl.multiple_of(start, TILE), size)


def dot(a, b, ca=1, cb=0):
    return lax.dot_general(a, b, (((ca,), (cb,)), ((), ())), preferred_element_type=jnp.float32)


def split_kernel(count, *refs):
    index_ref, out_ref, sems = refs[count], refs[-2], refs[-1]
    half = out_ref.shape[1]
    rows = refs[0].shape[0]
    side = (lax.axis_index("seq") + 1) % 2
    copies = []
    for at, ref in enumerate(refs[:count]):
        source = ref.at[:, lanes(side * half, half)]
        copies.append(pltpu.make_async_copy(source, out_ref.at[pl.ds(at * rows, rows), :], sems.at[at]))
    for copy in copies:
        copy.start()
    tail = out_ref.shape[0] - count * rows
    if tail:
        row = jnp.broadcast_to(index_ref[...].astype(jnp.float32), (tail, rows)).astype(jnp.bfloat16)
        out_ref[pl.ds(count * rows, tail), :] = jnp.zeros((tail, half), jnp.bfloat16)
        out_ref[pl.ds(count * rows, tail), pl.ds(0, rows)] = row
    for copy in copies:
        copy.wait()


def state_kernel(info, k_ref, v_ref, got_ref, sum_ref, send_ref, even_ref):
    heads, dim, _ = sum_ref.shape
    rows = k_ref.shape[0]
    core = info[0]
    for h in range(heads):
        far = pl.ds(h * dim, dim)
        own = lanes(core * heads * dim + h * dim, dim)
        mine = dot(v_ref[:, own], k_ref[:, own], 0, 0)
        theirs = dot(got_ref[pl.ds(rows, rows), far], got_ref[pl.ds(0, rows), far], 0, 0)
        both = mine + theirs
        sum_ref[h] = both
        send_ref[h] = both.astype(jnp.bfloat16)
        even_ref[h] = jnp.where(core == 0, mine, theirs).astype(jnp.bfloat16)


def local_kernel(own_side, info, lam_ref, *refs):
    out_ref = refs[-1]
    heads = lam_ref.shape[0]
    dim, rows = out_ref.shape[0] // heads, out_ref.shape[1]
    scale = 1.0 / math.sqrt(dim)
    step = min(TILE, rows)
    blocks = rows // step
    log_step = step.bit_length() - 1
    s_at = lax.broadcasted_iota(jnp.int32, (step, step), 0)
    t_at = lax.broadcasted_iota(jnp.int32, (step, step), 1)
    grid = jnp.zeros((step, step), jnp.int32)
    for bit in range(log_step):
        grid = grid + (jnp.right_shift(t_at, bit) != jnp.right_shift(s_at, bit)).astype(jnp.int32)
    grid = jnp.where(s_at <= t_at, grid, -1)
    for h in range(heads):

        def part(which, first, count):
            if own_side:
                return refs[which][pl.ds(first, count), lanes(info[0] * heads * dim + h * dim, dim)]
            ref, at = (refs[0], which * rows) if which < 2 else (refs[1], 0)
            return ref[pl.ds(at + first, count), pl.ds(h * dim, dim)]

        lam = lam_ref[h] * scale
        totals = [None] * blocks
        for s in range(blocks):
            scores = dot(part(0, s * step, step), part(2, s * step, rows - s * step), 1, 1)
            weighted = []
            for t in range(s, blocks):
                lam_t = lam[:, t * step : (t + 1) * step]
                if s == t:
                    picked = jnp.zeros((step, step), jnp.float32)
                    for level in range(log_step + 1):
                        picked = jnp.where(grid == level, lam_t[level : level + 1], picked)
                else:
                    level = log_step + (s ^ t).bit_length()
                    picked = lam_t[level : level + 1]
                weighted.append((picked * scores[:, (t - s) * step : (t - s + 1) * step]).astype(jnp.bfloat16))
            joined = weighted[0] if len(weighted) == 1 else jnp.concatenate(weighted, axis=1)
            add = dot(part(1, s * step, step), joined, 0, 0)
            for t in range(s, blocks):
                term = add[:, (t - s) * step : (t - s + 1) * step]
                totals[t] = term if totals[t] is None else totals[t] + term
        for t in range(blocks):
            out_ref[pl.ds(h * dim, dim), pl.ds(t * step, step)] = totals[t]


def early_kernel(levels, log_stretch, info, q_ref, got_ref, lam0_ref, lam1_ref, base0_ref, base1_ref, *refs):
    buckets, out_ref = refs[:-1], refs[-1]
    heads = lam0_ref.shape[0]
    rows = q_ref.shape[0]
    dim = base0_ref.shape[0] // heads
    core = info[0]
    scale = 1.0 / math.sqrt(dim)
    for h in range(heads):
        far = pl.ds(h * dim, dim)
        for side in range(2):
            odd = core if side == 0 else 1 - core
            lam = (lam0_ref, lam1_ref)[side][h]
            if side == 0:
                q = q_ref[:, lanes(core * heads * dim + h * dim, dim)]
            else:
                q = got_ref[pl.ds(0, rows), far]
            total = (base0_ref, base1_ref)[side][far, :]
            for at, level in enumerate(levels):
                column = log_stretch + 1 + level
                on = odd if level == 0 else info[1 + level]
                weight = jnp.where(on == 1, lam[column : column + 1] * scale, 0.0)
                total = total + weight * dot(buckets[at][h], q, 1, 1)
            out_ref[far, pl.ds(side * rows, rows)] = total


def last_kernel(levels, log_stretch, info, q_ref, got_ref, lam0_ref, lam1_ref, base_ref, gain_ref, *refs):
    buckets, out_ref = refs[:-1], refs[-1]
    heads = lam0_ref.shape[0]
    rows = q_ref.shape[0]
    dim = base_ref.shape[0] // heads
    core = info[0]
    scale = 1.0 / math.sqrt(dim)
    for h in range(heads):
        far = pl.ds(h * dim, dim)
        own = lanes(core * heads * dim + h * dim, dim)
        for side in range(2):
            at_rows = pl.ds(side * rows, rows)
            lam = (lam0_ref, lam1_ref)[side][h]
            if side == 0:
                q = q_ref[:, lanes(core * heads * dim + h * dim, dim)]
            else:
                q = got_ref[pl.ds(0, rows), far]
            total = base_ref[far, at_rows]
            for at, level in enumerate(levels):
                column = log_stretch + 1 + level
                weight = jnp.where(info[1 + level] == 1, lam[column : column + 1] * scale, 0.0)
                total = total + weight * dot(buckets[at][h], q, 1, 1)
            mean = jnp.mean(total * total, axis=0, keepdims=True)
            total = total * lax.rsqrt(mean + 1e-06)
            out_ref[at_rows, far] = (jnp.transpose(total) * gain_ref[:, own]).astype(out_ref.dtype)


def project_kernel(plan, info, normed_ref, *refs):
    pieces, own_ref, other_ref = refs[:-2], refs[-2], refs[-1]
    rows = own_ref.shape[0]
    for slot, (_, parts) in enumerate(plan):
        total = None
        for at, row0, k_slot, k_add, size in parts:
            start = k_add if k_slot is None else info[k_slot] + k_add
            term = dot(normed_ref[:, lanes(start, size)], pieces[at][pl.ds(row0, size), :])
            total = term if total is None else total + term
        width = pieces[parts[0][0]].shape[1]
        own_ref[:, pl.ds(slot * width, width)] = total[:rows]
        other_ref[:, pl.ds(slot * width, width)] = total[rows:].astype(other_ref.dtype)


def combine_kernel(plans, info, *refs):
    out_ref, held, sems = refs[-3:]
    copies = []
    for n, plan in enumerate(plans):
        own_ref, came_ref = refs[2 * n], refs[2 * n + 1]
        width = own_ref.shape[1] // len(plan)
        for slot, (chip_slot, _) in enumerate(plan):
            at = pl.ds(slot * width, width)
            column = 0 if chip_slot is None else info[chip_slot] * width
            total = own_ref[:, at] + came_ref[:, at].astype(jnp.float32)
            to = pl.ds(len(copies) * width, width)
            held[:, to] = total.astype(out_ref.dtype)
            copy = pltpu.make_async_copy(held.at[:, to], out_ref.at[:, lanes(column, width)], sems.at[len(copies)])
            copy.start()
            copies.append(copy)
    for copy in copies:
        copy.wait()


def ring_order(chips):
    return list(range(0, chips, 2)) + list(range(chips - 1, 0, -2))


def body(groups, queries, keys, values, level_index, level_table, norm_gain, out_weight):
    stretch, width = queries.shape
    table_rows, level_count, heads = level_table.shape
    head_dim = width // heads
    columns = out_weight.shape[1]
    log_stretch = stretch.bit_length() - 1
    devices = lax.axis_size("seq")
    log_blocks = devices.bit_length() - 1
    rank = lax.axis_index("seq")
    group = lax.axis_index("grp")
    core = rank % 2
    half = width // 2
    pair_heads = heads // 2
    chips = devices // 2
    ringed = (2 * columns) % TILE == 0 and chips >= 4
    shared = (3 * half // 8) // TILE * TILE if ringed and groups == 2 else 0
    kept = half - shared
    cut = kept // TILE // 2 * TILE

    order = ring_order(chips)
    facts = np.zeros((groups, devices, 1 + log_blocks + 2 + chips), np.int32)
    for g in range(groups):
        for r in range(devices):
            place = order.index(r // 2) if ringed else 0
            facts[g, r] = (
                [r % 2]
                + [r >> bit & 1 for bit in range(log_blocks)]
                + [g * shared, (1 - g) * kept]
                + [order[(place - d) % chips] if ringed else 0 for d in range(chips)]
            )
    k_mine, k_lacks, chip_at = 1 + log_blocks, 2 + log_blocks, 3 + log_blocks
    info = lax.dynamic_slice(jnp.asarray(facts), (group, rank, 0), (1, 1, facts.shape[2])).reshape(-1)

    def swap(block, bit, upward=False):
        route = [(r, r ^ 1 << bit) for r in range(devices) if not (upward and r >> bit & 1)]
        return lax.ppermute(block, "seq", route)

    packs = table_rows <= 256 and stretch <= half
    bf16 = functools.partial(jax.ShapeDtypeStruct, dtype=jnp.bfloat16)

    def split(arrays, tail, after):
        hbm = pl.BlockSpec(memory_space=pltpu.HBM)
        return pl.pallas_call(
            functools.partial(split_kernel, len(arrays)),
            out_shape=bf16((len(arrays) * stretch + tail, half)),
            in_specs=[hbm] * len(arrays) + [VM, pl.BlockSpec(memory_space=pl.ANY)],
            out_specs=VM,
            scratch_shapes=[pltpu.SemaphoreType.DMA((len(arrays),))],
            compiler_params=pltpu.CompilerParams(vmem_limit_bytes=56 * 1024 * 1024),
            cost_estimate=pl.CostEstimate(flops=us(2.0), bytes_accessed=1 << 20, transcendentals=0),
        )(*arrays, level_index.reshape(1, stretch), after)

    w_got = swap(out_weight, 0)
    got_kv = swap(split([keys, values], 0, level_index), 0)
    whole = jnp.where(
        core == 0,
        jnp.concatenate([out_weight[:half], w_got[:half]], axis=1),
        jnp.concatenate([w_got[half:], out_weight[half:]], axis=1),
    )

    got_q = swap(split([queries], 16 if packs else 0, whole), 0)
    if packs:
        index_got = got_q[stretch, :stretch].astype(jnp.int32)
    else:
        index_got = swap(level_index, 0)

    table = jnp.transpose(level_table, (2, 1, 0))
    table = jnp.where(core == 0, table[:pair_heads], table[pair_heads:]).reshape(-1, table_rows)

    def level_weights(index):
        found = (index[None, :] == jnp.arange(table_rows, dtype=jnp.int32)[:, None]).astype(jnp.float32)
        lam = jnp.dot(table, found, precision=lax.Precision.HIGHEST)
        return lam.reshape(pair_heads, level_count, stretch)

    lam_own = level_weights(level_index)
    lam_got = level_weights(index_got)

    state = jax.ShapeDtypeStruct((pair_heads, head_dim, head_dim), jnp.float32)
    state16 = jax.ShapeDtypeStruct(state.shape, jnp.bfloat16)
    total, send, even = call(
        state_kernel,
        (state, state16, state16),
        [SM] + [VM] * 3,
        us(1.0),
        1 << 20,
        info, keys, values, got_kv,
    )
    send_first = send
    buckets = [even]
    quarters = []
    reached = [send]
    upper = jnp.right_shift(rank, 1) % 2
    crossed = []

    def tie(x, *others):
        return lax.optimization_barrier((x, *others))[0]

    def level(bit):
        nonlocal total, send
        came = swap(send, bit)
        if bit + 1 < log_blocks:
            total = total + came
            if bit == 1:
                total = jnp.where(upper == 0, total[: pair_heads // 2], total[pair_heads // 2 :])
            send = total.astype(jnp.bfloat16)
            reached.append(send)
        if bit > 1:
            quarters.append(came)
        else:
            buckets.append(came)

    for bit in range(1, min(3, log_blocks)):
        level(bit)

    pieces = []
    plan = []
    middle, late = [], []
    landed = ()
    if ringed:
        clockwise = []
        for at, chip in enumerate(order):
            follows = order[(at + 1) % chips]
            clockwise += [(2 * chip + c, 2 * follows + c) for c in range(2)]
        counter = [(b, a) for a, b in clockwise]
        pieces.append(whole)
        plan.append((chip_at, [(0, 0, None, 0, half)]))
        right = left = jnp.where(group % 2 == 0, whole[:kept], whole[shared:]) if shared else whole
        rounds = chips // 2

        def ring_after(r):
            if r == 3:
                return reached[2:3] + crossed[:1]
            return []

        for r in range(1, rounds + 1):
            last = r == rounds
            right, left, *_ = lax.optimization_barrier((right, left, *ring_after(r)))
            if last:
                right, left = right[:cut], left[cut:]
            right = lax.ppermute(right, "seq", clockwise)
            left = lax.ppermute(left, "seq", counter)
            if r == 1:
                right, left, _ = lax.optimization_barrier((right, left, send_first))
            if r == 2:
                send = tie(send, right, left)
            at = len(pieces)
            pieces += [right, left]
            landed = (right, left)
            if last:
                parts = [[(at, 0, k_mine, 0, cut), (at + 1, 0, k_mine, cut, kept - cut)]]
                distances = [r]
            else:
                parts = [[(at, 0, k_mine, 0, kept)], [(at + 1, 0, k_mine, 0, kept)]]
                distances = [r, chips - r]
            if shared:
                held = [jnp.concatenate([right, left], axis=0)] if last else [right, left]
                low, high = ([x[at:][:shared] for x in held] for at in (0, kept - shared))
                wanted = jnp.where(group == 0, jnp.concatenate(low, axis=0), jnp.concatenate(high, axis=0))
                crossed.append(lax.ppermute(wanted, "grp", [(0, 1), (1, 0)]))
                pieces.append(crossed[-1])
                for n, part in enumerate(parts):
                    part.append((at + 2, n * shared, k_lacks, 0, shared))
            (plan if r < rounds - 1 else late if last else middle).extend(
                (chip_at + d, part) for d, part in zip(distances, parts)
            )
    else:
        full = lax.all_gather(out_weight, "seq", axis=1, tiled=True)
        pieces.append(lax.dynamic_slice(full, (core * half, 0), (half, width)))
        plan.append((None, [(0, 0, None, 0, half)]))

    while len(quarters) + 2 < log_blocks:
        level(len(quarters) + 2)
    joined = jnp.stack(quarters)
    rest = swap(joined, 1)
    both = jnp.where(
        upper == 0, jnp.concatenate([joined, rest], axis=1), jnp.concatenate([rest, joined], axis=1)
    )
    buckets += [both[n] for n in range(len(quarters))]

    side_shape = jax.ShapeDtypeStruct((half, stretch), jnp.float32)
    acc_own = call(
        functools.partial(local_kernel, True), side_shape, [SM] + [VM] * 4, us(2.1), 1 << 20,
        info, tie(lam_own, reached[0]), keys, values, queries,
    )
    acc_got = call(
        functools.partial(local_kernel, False), side_shape, [SM] + [VM] * 3, us(2.1), 1 << 20,
        info, tie(lam_got, reached[min(2, len(reached) - 1)]), got_kv, got_q,
    )
    acc = call(
        functools.partial(early_kernel, [0, 1], log_stretch),
        jax.ShapeDtypeStruct((half, 2 * stretch), jnp.float32),
        [SM] + [VM] * 8,
        us(1.6),
        1 << 20,
        info, queries, got_q, lam_own, lam_got, acc_own, acc_got, *buckets[:2],
    )
    normed = call(
        functools.partial(last_kernel, list(range(2, log_blocks)), log_stretch),
        jax.ShapeDtypeStruct((2 * stretch, half), jnp.bfloat16),
        [SM] + [VM] * (6 + len(quarters)),
        us(2.0),
        1 << 20,
        info, queries, got_q, lam_own, lam_got, acc, norm_gain.reshape(1, width), *buckets[2:],
    )

    plans = [p for p in (plan, middle, late) if p]
    shares = []
    for p in plans:
        used = sorted({part[0] for _, parts in p for part in parts})
        local = [(c, [(used.index(part[0]), *part[1:]) for part in parts]) for c, parts in p]
        wide = len(p) * pieces[used[0]].shape[1]
        own, other = call(
            functools.partial(project_kernel, local),
            (
                jax.ShapeDtypeStruct((stretch, wide), jnp.float32),
                jax.ShapeDtypeStruct((stretch, wide), jnp.bfloat16),
            ),
            [SM] + [VM] * (1 + len(used)),
            us(4.0 * wide / width),
            1 << 20,
            info, normed, *[pieces[n] for n in used],
        )
        shares += [own, swap(other, 0)]
    return pl.pallas_call(
        functools.partial(combine_kernel, plans),
        out_shape=jax.ShapeDtypeStruct((stretch, width), jnp.bfloat16),
        in_specs=[SM] + [VM] * len(shares),
        out_specs=pl.BlockSpec(memory_space=pltpu.HBM),
        scratch_shapes=[
            pltpu.VMEM((stretch, width), jnp.bfloat16),
            pltpu.SemaphoreType.DMA((sum(len(p) for p in plans),)),
        ],
        compiler_params=PARAMS,
        cost_estimate=pl.CostEstimate(flops=us(1.0), bytes_accessed=1 << 20, transcendentals=0),
    )(info, *shares)


def solution(mesh):
    placed = (
        P(("grp", "seq"), None),
        P(("grp", "seq"), None),
        P(("grp", "seq"), None),
        P(("grp", "seq")),
        P(),
        P(),
        P(None, "seq"),
    )
    return jax.shard_map(
        functools.partial(body, mesh.shape["grp"]),
        mesh=mesh,
        in_specs=placed,
        out_specs=P(("grp", "seq"), None),
        check_vma=False,
    )
```

```python
import functools
import math

import numpy as np

import jax
import jax.numpy as jnp
from jax import lax
from jax.experimental import pallas as pl
from jax.experimental.pallas import tpu as pltpu
from jax.sharding import PartitionSpec as P

TILE = 128
VM = pl.BlockSpec(memory_space=pltpu.VMEM)
SM = pl.BlockSpec(memory_space=pltpu.SMEM)
PARAMS = pltpu.CompilerParams(vmem_limit_bytes=8 * 1024 * 1024)


def call(kernel, out_shape, in_specs, flops, moved, *operands):
    outs = jax.tree.map(lambda _: VM, out_shape)
    return pl.pallas_call(
        kernel,
        out_shape=out_shape,
        in_specs=in_specs,
        out_specs=outs,
        compiler_params=PARAMS,
        cost_estimate=pl.CostEstimate(flops=flops, bytes_accessed=moved, transcendentals=0),
    )(*operands)


def us(microseconds):
    return int(microseconds * 1.15e9)


def lanes(start, size):
    return pl.ds(pl.multiple_of(start, TILE), size)


def dot(a, b, ca=1, cb=0):
    return lax.dot_general(a, b, (((ca,), (cb,)), ((), ())), preferred_element_type=jnp.float32)


def split_kernel(count, *refs):
    index_ref, out_ref, sems = refs[count], refs[-2], refs[-1]
    half = out_ref.shape[1]
    rows = refs[0].shape[0]
    side = (lax.axis_index("seq") + 1) % 2
    copies = []
    for at, ref in enumerate(refs[:count]):
        source = ref.at[:, lanes(side * half, half)]
        copies.append(pltpu.make_async_copy(source, out_ref.at[pl.ds(at * rows, rows), :], sems.at[at]))
    for copy in copies:
        copy.start()
    tail = out_ref.shape[0] - count * rows
    if tail:
        row = jnp.broadcast_to(index_ref[...].astype(jnp.float32), (tail, rows)).astype(jnp.bfloat16)
        out_ref[pl.ds(count * rows, tail), :] = jnp.zeros((tail, half), jnp.bfloat16)
        out_ref[pl.ds(count * rows, tail), pl.ds(0, rows)] = row
    for copy in copies:
        copy.wait()


def state_kernel(info, k_ref, v_ref, got_ref, sum_ref, send_ref, even_ref):
    heads, dim, _ = sum_ref.shape
    rows = k_ref.shape[0]
    core = info[0]
    for h in range(heads):
        far = pl.ds(h * dim, dim)
        own = lanes(core * heads * dim + h * dim, dim)
        mine = dot(v_ref[:, own], k_ref[:, own], 0, 0)
        theirs = dot(got_ref[pl.ds(rows, rows), far], got_ref[pl.ds(0, rows), far], 0, 0)
        both = mine + theirs
        sum_ref[h] = both
        send_ref[h] = both.astype(jnp.bfloat16)
        even_ref[h] = jnp.where(core == 0, mine, theirs).astype(jnp.bfloat16)


def local_kernel(own_side, info, lam_ref, *refs):
    out_ref = refs[-1]
    heads = lam_ref.shape[0]
    dim, rows = out_ref.shape[0] // heads, out_ref.shape[1]
    scale = 1.0 / math.sqrt(dim)
    step = min(TILE, rows)
    blocks = rows // step
    log_step = step.bit_length() - 1
    s_at = lax.broadcasted_iota(jnp.int32, (step, step), 0)
    t_at = lax.broadcasted_iota(jnp.int32, (step, step), 1)
    grid = jnp.zeros((step, step), jnp.int32)
    for bit in range(log_step):
        grid = grid + (jnp.right_shift(t_at, bit) != jnp.right_shift(s_at, bit)).astype(jnp.int32)
    grid = jnp.where(s_at <= t_at, grid, -1)
    for h in range(heads):

        def part(which, first, count):
            if own_side:
                return refs[which][pl.ds(first, count), lanes(info[0] * heads * dim + h * dim, dim)]
            ref, at = (refs[0], which * rows) if which < 2 else (refs[1], 0)
            return ref[pl.ds(at + first, count), pl.ds(h * dim, dim)]

        lam = lam_ref[h] * scale
        totals = [None] * blocks
        for s in range(blocks):
            scores = dot(part(0, s * step, step), part(2, s * step, rows - s * step), 1, 1)
            weighted = []
            for t in range(s, blocks):
                lam_t = lam[:, t * step : (t + 1) * step]
                if s == t:
                    picked = jnp.zeros((step, step), jnp.float32)
                    for level in range(log_step + 1):
                        picked = jnp.where(grid == level, lam_t[level : level + 1], picked)
                else:
                    level = log_step + (s ^ t).bit_length()
                    picked = lam_t[level : level + 1]
                weighted.append((picked * scores[:, (t - s) * step : (t - s + 1) * step]).astype(jnp.bfloat16))
            joined = weighted[0] if len(weighted) == 1 else jnp.concatenate(weighted, axis=1)
            add = dot(part(1, s * step, step), joined, 0, 0)
            for t in range(s, blocks):
                term = add[:, (t - s) * step : (t - s + 1) * step]
                totals[t] = term if totals[t] is None else totals[t] + term
        for t in range(blocks):
            out_ref[pl.ds(h * dim, dim), pl.ds(t * step, step)] = totals[t]


def early_kernel(levels, log_stretch, info, q_ref, got_ref, lam0_ref, lam1_ref, base0_ref, base1_ref, *refs):
    buckets, out_ref = refs[:-1], refs[-1]
    heads = lam0_ref.shape[0]
    rows = q_ref.shape[0]
    dim = base0_ref.shape[0] // heads
    core = info[0]
    scale = 1.0 / math.sqrt(dim)
    for h in range(heads):
        far = pl.ds(h * dim, dim)
        for side in range(2):
            odd = core if side == 0 else 1 - core
            lam = (lam0_ref, lam1_ref)[side][h]
            if side == 0:
                q = q_ref[:, lanes(core * heads * dim + h * dim, dim)]
            else:
                q = got_ref[pl.ds(0, rows), far]
            total = (base0_ref, base1_ref)[side][far, :]
            for at, level in enumerate(levels):
                column = log_stretch + 1 + level
                on = odd if level == 0 else info[1 + level]
                weight = jnp.where(on == 1, lam[column : column + 1] * scale, 0.0)
                total = total + weight * dot(buckets[at][h], q, 1, 1)
            out_ref[far, pl.ds(side * rows, rows)] = total


def last_kernel(levels, log_stretch, info, q_ref, got_ref, lam0_ref, lam1_ref, base_ref, gain_ref, *refs):
    buckets, out_ref = refs[:-1], refs[-1]
    heads = lam0_ref.shape[0]
    rows = q_ref.shape[0]
    dim = base_ref.shape[0] // heads
    core = info[0]
    scale = 1.0 / math.sqrt(dim)
    for h in range(heads):
        far = pl.ds(h * dim, dim)
        own = lanes(core * heads * dim + h * dim, dim)
        for side in range(2):
            at_rows = pl.ds(side * rows, rows)
            lam = (lam0_ref, lam1_ref)[side][h]
            if side == 0:
                q = q_ref[:, lanes(core * heads * dim + h * dim, dim)]
            else:
                q = got_ref[pl.ds(0, rows), far]
            total = base_ref[far, at_rows]
            for at, level in enumerate(levels):
                column = log_stretch + 1 + level
                weight = jnp.where(info[1 + level] == 1, lam[column : column + 1] * scale, 0.0)
                total = total + weight * dot(buckets[at][h], q, 1, 1)
            mean = jnp.mean(total * total, axis=0, keepdims=True)
            total = total * lax.rsqrt(mean + 1e-06)
            out_ref[at_rows, far] = (jnp.transpose(total) * gain_ref[:, own]).astype(out_ref.dtype)


def project_kernel(plan, info, normed_ref, *refs):
    pieces, own_ref, other_ref = refs[:-2], refs[-2], refs[-1]
    rows = own_ref.shape[0]
    for slot, (_, parts) in enumerate(plan):
        total = None
        for at, row0, k_slot, k_add, size in parts:
            start = k_add if k_slot is None else info[k_slot] + k_add
            term = dot(normed_ref[:, lanes(start, size)], pieces[at][pl.ds(row0, size), :])
            total = term if total is None else total + term
        width = pieces[parts[0][0]].shape[1]
        own_ref[:, pl.ds(slot * width, width)] = total[:rows]
        other_ref[:, pl.ds(slot * width, width)] = total[rows:].astype(other_ref.dtype)


def combine_kernel(plans, info, *refs):
    out_ref, held, sems = refs[-3:]
    copies = []
    for n, plan in enumerate(plans):
        own_ref, came_ref = refs[2 * n], refs[2 * n + 1]
        width = own_ref.shape[1] // len(plan)
        for slot, (chip_slot, _) in enumerate(plan):
            at = pl.ds(slot * width, width)
            column = 0 if chip_slot is None else info[chip_slot] * width
            total = own_ref[:, at] + came_ref[:, at].astype(jnp.float32)
            to = pl.ds(len(copies) * width, width)
            held[:, to] = total.astype(out_ref.dtype)
            copy = pltpu.make_async_copy(held.at[:, to], out_ref.at[:, lanes(column, width)], sems.at[len(copies)])
            copy.start()
            copies.append(copy)
    for copy in copies:
        copy.wait()


def ring_order(chips):
    return list(range(0, chips, 2)) + list(range(chips - 1, 0, -2))


def body(groups, queries, keys, values, level_index, level_table, norm_gain, out_weight):
    stretch, width = queries.shape
    table_rows, level_count, heads = level_table.shape
    head_dim = width // heads
    columns = out_weight.shape[1]
    log_stretch = stretch.bit_length() - 1
    devices = lax.axis_size("seq")
    log_blocks = devices.bit_length() - 1
    rank = lax.axis_index("seq")
    group = lax.axis_index("grp")
    core = rank % 2
    half = width // 2
    pair_heads = heads // 2
    chips = devices // 2
    ringed = (2 * columns) % TILE == 0 and chips >= 4
    shared = (3 * half // 8) // TILE * TILE if ringed and groups == 2 else 0
    kept = half - shared
    cut = kept // TILE // 2 * TILE

    order = ring_order(chips)
    facts = np.zeros((groups, devices, 1 + log_blocks + 2 + chips), np.int32)
    for g in range(groups):
        for r in range(devices):
            place = order.index(r // 2) if ringed else 0
            facts[g, r] = (
                [r % 2]
                + [r >> bit & 1 for bit in range(log_blocks)]
                + [g * shared, (1 - g) * kept]
                + [order[(place - d) % chips] if ringed else 0 for d in range(chips)]
            )
    k_mine, k_lacks, chip_at = 1 + log_blocks, 2 + log_blocks, 3 + log_blocks
    info = lax.dynamic_slice(jnp.asarray(facts), (group, rank, 0), (1, 1, facts.shape[2])).reshape(-1)

    def swap(block, bit, upward=False):
        route = [(r, r ^ 1 << bit) for r in range(devices) if not (upward and r >> bit & 1)]
        return lax.ppermute(block, "seq", route)

    packs = table_rows <= 256 and stretch <= half
    bf16 = functools.partial(jax.ShapeDtypeStruct, dtype=jnp.bfloat16)

    def split(arrays, tail, after):
        hbm = pl.BlockSpec(memory_space=pltpu.HBM)
        return pl.pallas_call(
            functools.partial(split_kernel, len(arrays)),
            out_shape=bf16((len(arrays) * stretch + tail, half)),
            in_specs=[hbm] * len(arrays) + [VM, pl.BlockSpec(memory_space=pl.ANY)],
            out_specs=VM,
            scratch_shapes=[pltpu.SemaphoreType.DMA((len(arrays),))],
            compiler_params=pltpu.CompilerParams(vmem_limit_bytes=56 * 1024 * 1024),
            cost_estimate=pl.CostEstimate(flops=us(2.0), bytes_accessed=1 << 20, transcendentals=0),
        )(*arrays, level_index.reshape(1, stretch), after)

    w_got = swap(out_weight, 0)
    got_kv = swap(split([keys, values], 0, level_index), 0)
    whole = jnp.where(
        core == 0,
        jnp.concatenate([out_weight[:half], w_got[:half]], axis=1),
        jnp.concatenate([w_got[half:], out_weight[half:]], axis=1),
    )

    got_q = swap(split([queries], 16 if packs else 0, whole), 0)
    if packs:
        index_got = got_q[stretch, :stretch].astype(jnp.int32)
    else:
        index_got = swap(level_index, 0)

    table = jnp.transpose(level_table, (2, 1, 0))
    table = jnp.where(core == 0, table[:pair_heads], table[pair_heads:]).reshape(-1, table_rows)

    def level_weights(index):
        found = (index[None, :] == jnp.arange(table_rows, dtype=jnp.int32)[:, None]).astype(jnp.float32)
        lam = jnp.dot(table, found, precision=lax.Precision.HIGHEST)
        return lam.reshape(pair_heads, level_count, stretch)

    lam_own = level_weights(level_index)
    lam_got = level_weights(index_got)

    state = jax.ShapeDtypeStruct((pair_heads, head_dim, head_dim), jnp.float32)
    state16 = jax.ShapeDtypeStruct(state.shape, jnp.bfloat16)
    total, send, even = call(
        state_kernel,
        (state, state16, state16),
        [SM] + [VM] * 3,
        us(1.0),
        1 << 20,
        info, keys, values, got_kv,
    )
    send_first = send
    buckets = [even]
    quarters = []
    reached = [send]
    upper = jnp.right_shift(rank, 1) % 2
    crossed = []

    def tie(x, *others):
        return lax.optimization_barrier((x, *others))[0]

    def level(bit):
        nonlocal total, send
        came = swap(send, bit)
        if bit + 1 < log_blocks:
            total = total + came
            if bit == 1:
                total = jnp.where(upper == 0, total[: pair_heads // 2], total[pair_heads // 2 :])
            send = total.astype(jnp.bfloat16)
            reached.append(send)
        if bit > 1:
            quarters.append(came)
        else:
            buckets.append(came)

    for bit in range(1, min(3, log_blocks)):
        level(bit)

    pieces = []
    plan = []
    middle, late = [], []
    landed = ()
    if ringed:
        clockwise = []
        for at, chip in enumerate(order):
            follows = order[(at + 1) % chips]
            clockwise += [(2 * chip + c, 2 * follows + c) for c in range(2)]
        counter = [(b, a) for a, b in clockwise]
        pieces.append(whole)
        plan.append((chip_at, [(0, 0, None, 0, half)]))
        right = left = jnp.where(group % 2 == 0, whole[:kept], whole[shared:]) if shared else whole
        rounds = chips // 2

        def ring_after(r):
            if r == 3:
                return reached[2:3] + crossed[:1]
            if r == 4:
                return crossed[1:2]
            return []

        for r in range(1, rounds + 1):
            last = r == rounds
            right, left, *_ = lax.optimization_barrier((right, left, *ring_after(r)))
            if last:
                right, left = right[:cut], left[cut:]
            right = lax.ppermute(right, "seq", clockwise)
            left = lax.ppermute(left, "seq", counter)
            if r == 1:
                right, left, _ = lax.optimization_barrier((right, left, send_first))
            if r == 2:
                send = tie(send, right, left)
            at = len(pieces)
            pieces += [right, left]
            landed = (right, left)
            if last:
                parts = [[(at, 0, k_mine, 0, cut), (at + 1, 0, k_mine, cut, kept - cut)]]
                distances = [r]
            else:
                parts = [[(at, 0, k_mine, 0, kept)], [(at + 1, 0, k_mine, 0, kept)]]
                distances = [r, chips - r]
            if shared:
                held = [jnp.concatenate([right, left], axis=0)] if last else [right, left]
                low, high = ([x[at:][:shared] for x in held] for at in (0, kept - shared))
                wanted = jnp.where(group == 0, jnp.concatenate(low, axis=0), jnp.concatenate(high, axis=0))
                crossed.append(lax.ppermute(wanted, "grp", [(0, 1), (1, 0)]))
                pieces.append(crossed[-1])
                for n, part in enumerate(parts):
                    part.append((at + 2, n * shared, k_lacks, 0, shared))
            (plan if r < rounds - 1 else late if last else middle).extend(
                (chip_at + d, part) for d, part in zip(distances, parts)
            )
    else:
        full = lax.all_gather(out_weight, "seq", axis=1, tiled=True)
        pieces.append(lax.dynamic_slice(full, (core * half, 0), (half, width)))
        plan.append((None, [(0, 0, None, 0, half)]))

    while len(quarters) + 2 < log_blocks:
        level(len(quarters) + 2)
    joined = jnp.stack(quarters)
    rest = swap(joined, 1)
    both = jnp.where(
        upper == 0, jnp.concatenate([joined, rest], axis=1), jnp.concatenate([rest, joined], axis=1)
    )
    buckets += [both[n] for n in range(len(quarters))]

    side_shape = jax.ShapeDtypeStruct((half, stretch), jnp.float32)
    acc_own = call(
        functools.partial(local_kernel, True), side_shape, [SM] + [VM] * 4, us(2.1), 1 << 20,
        info, tie(lam_own, reached[1]), keys, values, queries,
    )
    acc_got = call(
        functools.partial(local_kernel, False), side_shape, [SM] + [VM] * 3, us(2.1), 1 << 20,
        info, tie(lam_got, reached[min(2, len(reached) - 1)]), got_kv, got_q,
    )
    acc = call(
        functools.partial(early_kernel, [0, 1], log_stretch),
        jax.ShapeDtypeStruct((half, 2 * stretch), jnp.float32),
        [SM] + [VM] * 8,
        us(1.6),
        1 << 20,
        info, queries, got_q, lam_own, lam_got, acc_own, acc_got, *buckets[:2],
    )
    normed = call(
        functools.partial(last_kernel, list(range(2, log_blocks)), log_stretch),
        jax.ShapeDtypeStruct((2 * stretch, half), jnp.bfloat16),
        [SM] + [VM] * (6 + len(quarters)),
        us(2.0),
        1 << 20,
        info, queries, got_q, lam_own, lam_got, acc, norm_gain.reshape(1, width), *buckets[2:],
    )

    plans = [p for p in (plan, middle, late) if p]
    shares = []
    for p in plans:
        used = sorted({part[0] for _, parts in p for part in parts})
        local = [(c, [(used.index(part[0]), *part[1:]) for part in parts]) for c, parts in p]
        wide = len(p) * pieces[used[0]].shape[1]
        own, other = call(
            functools.partial(project_kernel, local),
            (
                jax.ShapeDtypeStruct((stretch, wide), jnp.float32),
                jax.ShapeDtypeStruct((stretch, wide), jnp.bfloat16),
            ),
            [SM] + [VM] * (1 + len(used)),
            us(4.0 * wide / width),
            1 << 20,
            info, normed, *[pieces[n] for n in used],
        )
        shares += [own, swap(other, 0)]
    return pl.pallas_call(
        functools.partial(combine_kernel, plans),
        out_shape=jax.ShapeDtypeStruct((stretch, width), jnp.bfloat16),
        in_specs=[SM] + [VM] * len(shares),
        out_specs=pl.BlockSpec(memory_space=pltpu.HBM),
        scratch_shapes=[
            pltpu.VMEM((stretch, width), jnp.bfloat16),
            pltpu.SemaphoreType.DMA((sum(len(p) for p in plans),)),
        ],
        compiler_params=PARAMS,
        cost_estimate=pl.CostEstimate(flops=us(1.0), bytes_accessed=1 << 20, transcendentals=0),
    )(info, *shares)


def solution(mesh):
    placed = (
        P(("grp", "seq"), None),
        P(("grp", "seq"), None),
        P(("grp", "seq"), None),
        P(("grp", "seq")),
        P(),
        P(),
        P(None, "seq"),
    )
    return jax.shard_map(
        functools.partial(body, mesh.shape["grp"]),
        mesh=mesh,
        in_specs=placed,
        out_specs=P(("grp", "seq"), None),
        check_vma=False,
    )
```

```python
import functools
import math

import numpy as np

import jax
import jax.numpy as jnp
from jax import lax
from jax.experimental import pallas as pl
from jax.experimental.pallas import tpu as pltpu
from jax.sharding import PartitionSpec as P

TILE = 128
VM = pl.BlockSpec(memory_space=pltpu.VMEM)
SM = pl.BlockSpec(memory_space=pltpu.SMEM)
PARAMS = pltpu.CompilerParams(vmem_limit_bytes=8 * 1024 * 1024)


def call(kernel, out_shape, in_specs, flops, moved, *operands):
    outs = jax.tree.map(lambda _: VM, out_shape)
    return pl.pallas_call(
        kernel,
        out_shape=out_shape,
        in_specs=in_specs,
        out_specs=outs,
        compiler_params=PARAMS,
        cost_estimate=pl.CostEstimate(flops=flops, bytes_accessed=moved, transcendentals=0),
    )(*operands)


def us(microseconds):
    return int(microseconds * 1.15e9)


def lanes(start, size):
    return pl.ds(pl.multiple_of(start, TILE), size)


def dot(a, b, ca=1, cb=0):
    return lax.dot_general(a, b, (((ca,), (cb,)), ((), ())), preferred_element_type=jnp.float32)


def split_kernel(count, *refs):
    index_ref, out_ref, sems = refs[count], refs[-2], refs[-1]
    half = out_ref.shape[1]
    rows = refs[0].shape[0]
    side = (lax.axis_index("seq") + 1) % 2
    copies = []
    for at, ref in enumerate(refs[:count]):
        source = ref.at[:, lanes(side * half, half)]
        copies.append(pltpu.make_async_copy(source, out_ref.at[pl.ds(at * rows, rows), :], sems.at[at]))
    for copy in copies:
        copy.start()
    tail = out_ref.shape[0] - count * rows
    if tail:
        row = jnp.broadcast_to(index_ref[...].astype(jnp.float32), (tail, rows)).astype(jnp.bfloat16)
        out_ref[pl.ds(count * rows, tail), :] = jnp.zeros((tail, half), jnp.bfloat16)
        out_ref[pl.ds(count * rows, tail), pl.ds(0, rows)] = row
    for copy in copies:
        copy.wait()


def state_kernel(info, k_ref, v_ref, got_ref, sum_ref, send_ref, even_ref):
    heads, dim, _ = sum_ref.shape
    rows = k_ref.shape[0]
    core = info[0]
    for h in range(heads):
        far = pl.ds(h * dim, dim)
        own = lanes(core * heads * dim + h * dim, dim)
        mine = dot(v_ref[:, own], k_ref[:, own], 0, 0)
        theirs = dot(got_ref[pl.ds(rows, rows), far], got_ref[pl.ds(0, rows), far], 0, 0)
        both = mine + theirs
        sum_ref[h] = both
        send_ref[h] = both.astype(jnp.bfloat16)
        even_ref[h] = jnp.where(core == 0, mine, theirs).astype(jnp.bfloat16)


def local_kernel(own_side, info, lam_ref, *refs):
    out_ref = refs[-1]
    heads = lam_ref.shape[0]
    dim, rows = out_ref.shape[0] // heads, out_ref.shape[1]
    scale = 1.0 / math.sqrt(dim)
    step = min(TILE, rows)
    blocks = rows // step
    log_step = step.bit_length() - 1
    s_at = lax.broadcasted_iota(jnp.int32, (step, step), 0)
    t_at = lax.broadcasted_iota(jnp.int32, (step, step), 1)
    grid = jnp.zeros((step, step), jnp.int32)
    for bit in range(log_step):
        grid = grid + (jnp.right_shift(t_at, bit) != jnp.right_shift(s_at, bit)).astype(jnp.int32)
    grid = jnp.where(s_at <= t_at, grid, -1)
    for h in range(heads):

        def part(which, first, count):
            if own_side:
                return refs[which][pl.ds(first, count), lanes(info[0] * heads * dim + h * dim, dim)]
            ref, at = (refs[0], which * rows) if which < 2 else (refs[1], 0)
            return ref[pl.ds(at + first, count), pl.ds(h * dim, dim)]

        lam = lam_ref[h] * scale
        totals = [None] * blocks
        for s in range(blocks):
            scores = dot(part(0, s * step, step), part(2, s * step, rows - s * step), 1, 1)
            weighted = []
            for t in range(s, blocks):
                lam_t = lam[:, t * step : (t + 1) * step]
                if s == t:
                    picked = jnp.zeros((step, step), jnp.float32)
                    for level in range(log_step + 1):
                        picked = jnp.where(grid == level, lam_t[level : level + 1], picked)
                else:
                    level = log_step + (s ^ t).bit_length()
                    picked = lam_t[level : level + 1]
                weighted.append((picked * scores[:, (t - s) * step : (t - s + 1) * step]).astype(jnp.bfloat16))
            joined = weighted[0] if len(weighted) == 1 else jnp.concatenate(weighted, axis=1)
            add = dot(part(1, s * step, step), joined, 0, 0)
            for t in range(s, blocks):
                term = add[:, (t - s) * step : (t - s + 1) * step]
                totals[t] = term if totals[t] is None else totals[t] + term
        for t in range(blocks):
            out_ref[pl.ds(h * dim, dim), pl.ds(t * step, step)] = totals[t]


def early_kernel(levels, log_stretch, info, q_ref, got_ref, lam0_ref, lam1_ref, base0_ref, base1_ref, *refs):
    buckets, out_ref = refs[:-1], refs[-1]
    heads = lam0_ref.shape[0]
    rows = q_ref.shape[0]
    dim = base0_ref.shape[0] // heads
    core = info[0]
    scale = 1.0 / math.sqrt(dim)
    for h in range(heads):
        far = pl.ds(h * dim, dim)
        for side in range(2):
            odd = core if side == 0 else 1 - core
            lam = (lam0_ref, lam1_ref)[side][h]
            if side == 0:
                q = q_ref[:, lanes(core * heads * dim + h * dim, dim)]
            else:
                q = got_ref[pl.ds(0, rows), far]
            total = (base0_ref, base1_ref)[side][far, :]
            for at, level in enumerate(levels):
                column = log_stretch + 1 + level
                on = odd if level == 0 else info[1 + level]
                weight = jnp.where(on == 1, lam[column : column + 1] * scale, 0.0)
                total = total + weight * dot(buckets[at][h], q, 1, 1)
            out_ref[far, pl.ds(side * rows, rows)] = total


def last_kernel(levels, log_stretch, info, q_ref, got_ref, lam0_ref, lam1_ref, base_ref, gain_ref, *refs):
    buckets, out_ref = refs[:-1], refs[-1]
    heads = lam0_ref.shape[0]
    rows = q_ref.shape[0]
    dim = base_ref.shape[0] // heads
    core = info[0]
    scale = 1.0 / math.sqrt(dim)
    for h in range(heads):
        far = pl.ds(h * dim, dim)
        own = lanes(core * heads * dim + h * dim, dim)
        for side in range(2):
            at_rows = pl.ds(side * rows, rows)
            lam = (lam0_ref, lam1_ref)[side][h]
            if side == 0:
                q = q_ref[:, lanes(core * heads * dim + h * dim, dim)]
            else:
                q = got_ref[pl.ds(0, rows), far]
            total = base_ref[far, at_rows]
            for at, level in enumerate(levels):
                column = log_stretch + 1 + level
                weight = jnp.where(info[1 + level] == 1, lam[column : column + 1] * scale, 0.0)
                total = total + weight * dot(buckets[at][h], q, 1, 1)
            mean = jnp.mean(total * total, axis=0, keepdims=True)
            total = total * lax.rsqrt(mean + 1e-06)
            out_ref[at_rows, far] = (jnp.transpose(total) * gain_ref[:, own]).astype(out_ref.dtype)


def project_kernel(plan, info, normed_ref, *refs):
    pieces, own_ref, other_ref = refs[:-2], refs[-2], refs[-1]
    rows = own_ref.shape[0]
    for slot, (_, parts) in enumerate(plan):
        total = None
        for at, row0, k_slot, k_add, size in parts:
            start = k_add if k_slot is None else info[k_slot] + k_add
            term = dot(normed_ref[:, lanes(start, size)], pieces[at][pl.ds(row0, size), :])
            total = term if total is None else total + term
        width = pieces[parts[0][0]].shape[1]
        own_ref[:, pl.ds(slot * width, width)] = total[:rows]
        other_ref[:, pl.ds(slot * width, width)] = total[rows:].astype(other_ref.dtype)


def combine_kernel(plans, info, *refs):
    out_ref, held, sems = refs[-3:]
    copies = []
    for n, plan in enumerate(plans):
        own_ref, came_ref = refs[2 * n], refs[2 * n + 1]
        width = own_ref.shape[1] // len(plan)
        for slot, (chip_slot, _) in enumerate(plan):
            at = pl.ds(slot * width, width)
            column = 0 if chip_slot is None else info[chip_slot] * width
            total = own_ref[:, at] + came_ref[:, at].astype(jnp.float32)
            to = pl.ds(len(copies) * width, width)
            held[:, to] = total.astype(out_ref.dtype)
            copy = pltpu.make_async_copy(held.at[:, to], out_ref.at[:, lanes(column, width)], sems.at[len(copies)])
            copy.start()
            copies.append(copy)
    for copy in copies:
        copy.wait()


def ring_order(chips):
    return list(range(0, chips, 2)) + list(range(chips - 1, 0, -2))


def body(groups, queries, keys, values, level_index, level_table, norm_gain, out_weight):
    stretch, width = queries.shape
    table_rows, level_count, heads = level_table.shape
    head_dim = width // heads
    columns = out_weight.shape[1]
    log_stretch = stretch.bit_length() - 1
    devices = lax.axis_size("seq")
    log_blocks = devices.bit_length() - 1
    rank = lax.axis_index("seq")
    group = lax.axis_index("grp")
    core = rank % 2
    half = width // 2
    pair_heads = heads // 2
    chips = devices // 2
    ringed = (2 * columns) % TILE == 0 and chips >= 4
    shared = (3 * half // 8) // TILE * TILE if ringed and groups == 2 else 0
    kept = half - shared
    cut = kept // TILE // 2 * TILE

    order = ring_order(chips)
    facts = np.zeros((groups, devices, 1 + log_blocks + 2 + chips), np.int32)
    for g in range(groups):
        for r in range(devices):
            place = order.index(r // 2) if ringed else 0
            facts[g, r] = (
                [r % 2]
                + [r >> bit & 1 for bit in range(log_blocks)]
                + [g * shared, (1 - g) * kept]
                + [order[(place - d) % chips] if ringed else 0 for d in range(chips)]
            )
    k_mine, k_lacks, chip_at = 1 + log_blocks, 2 + log_blocks, 3 + log_blocks
    info = lax.dynamic_slice(jnp.asarray(facts), (group, rank, 0), (1, 1, facts.shape[2])).reshape(-1)

    def swap(block, bit, upward=False):
        route = [(r, r ^ 1 << bit) for r in range(devices) if not (upward and r >> bit & 1)]
        return lax.ppermute(block, "seq", route)

    packs = table_rows <= 256 and stretch <= half
    bf16 = functools.partial(jax.ShapeDtypeStruct, dtype=jnp.bfloat16)

    def split(arrays, tail, after):
        hbm = pl.BlockSpec(memory_space=pltpu.HBM)
        return pl.pallas_call(
            functools.partial(split_kernel, len(arrays)),
            out_shape=bf16((len(arrays) * stretch + tail, half)),
            in_specs=[hbm] * len(arrays) + [VM, pl.BlockSpec(memory_space=pl.ANY)],
            out_specs=VM,
            scratch_shapes=[pltpu.SemaphoreType.DMA((len(arrays),))],
            compiler_params=pltpu.CompilerParams(vmem_limit_bytes=56 * 1024 * 1024),
            cost_estimate=pl.CostEstimate(flops=us(2.0), bytes_accessed=1 << 20, transcendentals=0),
        )(*arrays, level_index.reshape(1, stretch), after)

    w_got = swap(out_weight, 0)
    got_kv = swap(split([keys, values], 0, level_index), 0)
    whole = jnp.where(
        core == 0,
        jnp.concatenate([out_weight[:half], w_got[:half]], axis=1),
        jnp.concatenate([w_got[half:], out_weight[half:]], axis=1),
    )

    got_q = swap(split([queries], 16 if packs else 0, whole), 0)
    if packs:
        index_got = got_q[stretch, :stretch].astype(jnp.int32)
    else:
        index_got = swap(level_index, 0)

    table = jnp.transpose(level_table, (2, 1, 0))
    table = jnp.where(core == 0, table[:pair_heads], table[pair_heads:]).reshape(-1, table_rows)

    def level_weights(index):
        found = (index[None, :] == jnp.arange(table_rows, dtype=jnp.int32)[:, None]).astype(jnp.float32)
        lam = jnp.dot(table, found, precision=lax.Precision.HIGHEST)
        return lam.reshape(pair_heads, level_count, stretch)

    lam_own = level_weights(level_index)
    lam_got = level_weights(index_got)

    state = jax.ShapeDtypeStruct((pair_heads, head_dim, head_dim), jnp.float32)
    state16 = jax.ShapeDtypeStruct(state.shape, jnp.bfloat16)
    total, send, even = call(
        state_kernel,
        (state, state16, state16),
        [SM] + [VM] * 3,
        us(1.0),
        1 << 20,
        info, keys, values, got_kv,
    )
    send_first = send
    buckets = [even]
    quarters = []
    reached = [send]
    upper = jnp.right_shift(rank, 1) % 2
    crossed = []

    def tie(x, *others):
        return lax.optimization_barrier((x, *others))[0]

    def level(bit):
        nonlocal total, send
        came = swap(send, bit)
        if bit + 1 < log_blocks:
            total = total + came
            if bit == 1:
                total = jnp.where(upper == 0, total[: pair_heads // 2], total[pair_heads // 2 :])
            send = total.astype(jnp.bfloat16)
            reached.append(send)
        if bit > 1:
            quarters.append(came)
        else:
            buckets.append(came)

    for bit in range(1, min(3, log_blocks)):
        level(bit)

    pieces = []
    plan = []
    middle, late = [], []
    landed = ()
    if ringed:
        clockwise = []
        for at, chip in enumerate(order):
            follows = order[(at + 1) % chips]
            clockwise += [(2 * chip + c, 2 * follows + c) for c in range(2)]
        counter = [(b, a) for a, b in clockwise]
        pieces.append(whole)
        plan.append((chip_at, [(0, 0, None, 0, half)]))
        right = left = jnp.where(group % 2 == 0, whole[:kept], whole[shared:]) if shared else whole
        rounds = chips // 2

        def ring_after(r):
            if r == 3:
                return reached[2:3] + crossed[:1]
            if r == 4:
                return crossed[1:2]
            return []

        for r in range(1, rounds + 1):
            last = r == rounds
            right, left, *_ = lax.optimization_barrier((right, left, *ring_after(r)))
            if last:
                right, left = right[:cut], left[cut:]
            right = lax.ppermute(right, "seq", clockwise)
            left = lax.ppermute(left, "seq", counter)
            if r == 1:
                right, left, _ = lax.optimization_barrier((right, left, send_first))
            if r == 2:
                send = tie(send, right, left)
            at = len(pieces)
            pieces += [right, left]
            landed = (right, left)
            if last:
                parts = [[(at, 0, k_mine, 0, cut), (at + 1, 0, k_mine, cut, kept - cut)]]
                distances = [r]
            else:
                parts = [[(at, 0, k_mine, 0, kept)], [(at + 1, 0, k_mine, 0, kept)]]
                distances = [r, chips - r]
            if shared:
                held = [jnp.concatenate([right, left], axis=0)] if last else [right, left]
                low, high = ([x[at:][:shared] for x in held] for at in (0, kept - shared))
                wanted = jnp.where(group == 0, jnp.concatenate(low, axis=0), jnp.concatenate(high, axis=0))
                crossed.append(lax.ppermute(wanted, "grp", [(0, 1), (1, 0)]))
                pieces.append(crossed[-1])
                for n, part in enumerate(parts):
                    part.append((at + 2, n * shared, k_lacks, 0, shared))
            (plan if r < rounds - 1 else late if last else middle).extend(
                (chip_at + d, part) for d, part in zip(distances, parts)
            )
    else:
        full = lax.all_gather(out_weight, "seq", axis=1, tiled=True)
        pieces.append(lax.dynamic_slice(full, (core * half, 0), (half, width)))
        plan.append((None, [(0, 0, None, 0, half)]))

    while len(quarters) + 2 < log_blocks:
        level(len(quarters) + 2)
    joined = tie(jnp.stack(quarters), *crossed[1:2])
    rest = swap(joined, 1)
    both = jnp.where(
        upper == 0, jnp.concatenate([joined, rest], axis=1), jnp.concatenate([rest, joined], axis=1)
    )
    buckets += [both[n] for n in range(len(quarters))]

    side_shape = jax.ShapeDtypeStruct((half, stretch), jnp.float32)
    acc_own = call(
        functools.partial(local_kernel, True), side_shape, [SM] + [VM] * 4, us(2.1), 1 << 20,
        info, tie(lam_own, reached[1]), keys, values, queries,
    )
    acc_got = call(
        functools.partial(local_kernel, False), side_shape, [SM] + [VM] * 3, us(2.1), 1 << 20,
        info, tie(lam_got, reached[min(2, len(reached) - 1)]), got_kv, got_q,
    )
    acc = call(
        functools.partial(early_kernel, [0, 1], log_stretch),
        jax.ShapeDtypeStruct((half, 2 * stretch), jnp.float32),
        [SM] + [VM] * 8,
        us(1.6),
        1 << 20,
        info, queries, got_q, lam_own, lam_got, acc_own, acc_got, *buckets[:2],
    )
    normed = call(
        functools.partial(last_kernel, list(range(2, log_blocks)), log_stretch),
        jax.ShapeDtypeStruct((2 * stretch, half), jnp.bfloat16),
        [SM] + [VM] * (6 + len(quarters)),
        us(2.0),
        1 << 20,
        info, queries, got_q, lam_own, lam_got, acc, norm_gain.reshape(1, width), *buckets[2:],
    )

    plans = [p for p in (plan, middle, late) if p]
    shares = []
    for p in plans:
        used = sorted({part[0] for _, parts in p for part in parts})
        local = [(c, [(used.index(part[0]), *part[1:]) for part in parts]) for c, parts in p]
        wide = len(p) * pieces[used[0]].shape[1]
        own, other = call(
            functools.partial(project_kernel, local),
            (
                jax.ShapeDtypeStruct((stretch, wide), jnp.float32),
                jax.ShapeDtypeStruct((stretch, wide), jnp.bfloat16),
            ),
            [SM] + [VM] * (1 + len(used)),
            us(4.0 * wide / width),
            1 << 20,
            info, normed, *[pieces[n] for n in used],
        )
        shares += [own, swap(other, 0)]
    return pl.pallas_call(
        functools.partial(combine_kernel, plans),
        out_shape=jax.ShapeDtypeStruct((stretch, width), jnp.bfloat16),
        in_specs=[SM] + [VM] * len(shares),
        out_specs=pl.BlockSpec(memory_space=pltpu.HBM),
        scratch_shapes=[
            pltpu.VMEM((stretch, width), jnp.bfloat16),
            pltpu.SemaphoreType.DMA((sum(len(p) for p in plans),)),
        ],
        compiler_params=PARAMS,
        cost_estimate=pl.CostEstimate(flops=us(1.0), bytes_accessed=1 << 20, transcendentals=0),
    )(info, *shares)


def solution(mesh):
    placed = (
        P(("grp", "seq"), None),
        P(("grp", "seq"), None),
        P(("grp", "seq"), None),
        P(("grp", "seq")),
        P(),
        P(),
        P(None, "seq"),
    )
    return jax.shard_map(
        functools.partial(body, mesh.shape["grp"]),
        mesh=mesh,
        in_specs=placed,
        out_specs=P(("grp", "seq"), None),
        check_vma=False,
    )
```
